128 devices in a mesh: span: 16 (over z, y), chord: 8 (over x, core).
Axes of the slice: x: 4, y: 4, z: 4, core: 2. Of those that a mesh axis runs over, the one named last changes fastest.
Arguments:
- query_tiles: bfloat16 [32, 16, 128, 512], P('span', 'chord'), may hold values from -67 to 67
- key_tiles: bfloat16 [32, 16, 128, 512], P('span', 'chord'), may hold values from -6 to 6
- value_tiles: bfloat16 [32, 16, 128, 512], P('span', 'chord'), may hold values from -6 to 6
- out_grad: bfloat16 [32, 16, 128, 512], P('span', 'chord'), may hold values from -6 to 6
- mix_gain: float32 [4, 512], replicated, may hold values from 0.1 to 0.8
- partners: int32 [32, 16, 8], P('span', 'chord'), may hold values from 0 to 511, as said below
- counts: int32 [32, 16], P('span', 'chord'), may hold values from 1 to 8
Outputs:
- query_grad: bfloat16 [32, 16, 128, 512], P('span', 'chord')
- key_grad: bfloat16 [32, 16, 128, 512], P('span', 'chord')
- value_grad: bfloat16 [32, 16, 128, 512], P('span', 'chord')
The draws below stay inside these ranges and needn't reach their ends.
Inputs may be any that keep to these rules, and one draw needn't show every extreme that they name: `partners`: slot j of a patch's list, for j below its count, is the flattened index (span position times 16 plus chord position) of a distinct patch at most one step away along each grid dimension; slot 0 is the patch itself; slots at or past the count hold the patch's own index.
All inputs are finite; a program needn't handle non-finite values.
Results may differ from the reference program's by a relative error of at most 0.012.
The reference program's roundings to bfloat16 on the way count: a program that leaves them out, or rounds other values in their place, can miss the bound.
Values may be sent and summed in bfloat16 or wider, within the bound.
No kernel may reach another device: no remote copies, remote signals or barrier semaphores. Data moves between devices by JAX's collectives and lax.ppermute only.
A program may use at most 128 MiB of HBM per device.

```python
import math
import jax
import jax.numpy as jnp
from jax import lax

D = 512
HEADS = 8
PATCH = 128
MAXP = 8
PS_ALL = 32
PC_ALL = 16


def drawn_pair(key):
    grid_shape = (PS_ALL, PC_ALL, PATCH, D)
    key_rows = jnp.clip(jax.random.normal(jax.random.fold_in(key, 21), grid_shape, jnp.float32), -6.0, 6.0)
    query_rows = jnp.clip(jax.random.normal(jax.random.fold_in(key, 22), grid_shape, jnp.float32), -6.0, 6.0)
    return (query_rows, key_rows)


def draw_query_tiles(key, part):
    return drawn_pair(key)[0].astype(jnp.bfloat16)


def draw_key_tiles(key, part):
    return drawn_pair(key)[1].astype(jnp.bfloat16)


def partner_tables(key):
    table_key = jax.random.fold_in(key, 31)
    grid_shape = (PS_ALL, PC_ALL, 8)
    span_at = lax.broadcasted_iota(jnp.int32, grid_shape, 0)
    chord_at = lax.broadcasted_iota(jnp.int32, grid_shape, 1)
    slot_at = lax.broadcasted_iota(jnp.int32, grid_shape, 2)
    span_steps = jnp.array([-1, -1, -1, 0, 0, 1, 1, 1], jnp.int32)
    chord_steps = jnp.array([-1, 0, 1, -1, 1, -1, 0, 1], jnp.int32)
    near_span = span_at + span_steps
    near_chord = chord_at + chord_steps
    inside = (near_span >= 0) & (near_span < PS_ALL) & (near_chord >= 0) & (near_chord < PC_ALL)
    ranking = jax.random.randint(jax.random.fold_in(table_key, 1), grid_shape, 0, 4096) * 8 + slot_at
    ranking = jnp.where(inside, ranking, ranking + 65536)
    ranked = jnp.argsort(ranking, axis=-1)
    near_ids = jnp.take_along_axis(near_span * PC_ALL + near_chord, ranked, axis=-1)
    inside_count = jnp.sum(inside.astype(jnp.int32), axis=-1)
    drawn = jax.random.randint(jax.random.fold_in(table_key, 2), (PS_ALL, PC_ALL), 0, MAXP)
    list_counts = 1 + jnp.minimum(drawn, inside_count)
    own_id = span_at[:, :, 0] * PC_ALL + chord_at[:, :, 0]
    slot_ids = jnp.concatenate([own_id[:, :, None], near_ids[:, :, :MAXP - 1]], axis=-1)
    live_slot = lax.broadcasted_iota(jnp.int32, (PS_ALL, PC_ALL, MAXP), 2) < list_counts[:, :, None]
    partner_ids = jnp.where(live_slot, slot_ids, own_id[:, :, None])
    return (partner_ids.astype(jnp.int32), list_counts.astype(jnp.int32))


def draw_partners(key, part):
    return partner_tables(key)[0]


def draw_counts(key, part):
    return partner_tables(key)[1]


def block_scale(stream_key, extent, shards, smallest, largest):
    factor_of = 1.0
    for dim, blocks in shards:
        steps = jax.random.uniform(jax.random.fold_in(jax.random.fold_in(stream_key, 6), dim), (blocks,), jnp.float32, smallest / len(shards), largest / len(shards))
        factor_of = factor_of * jnp.repeat(jnp.exp(steps), extent[dim] // blocks).reshape((-1,) + (1,) * (len(extent) - 1 - dim))
    return factor_of


def gaussian(key, shape, scale, bound, shards=(), kind=jnp.bfloat16):
    values = scale * jax.random.normal(key, shape, jnp.float32)
    if shards:
        values = values * block_scale(key, shape, shards, -0.22, 0.18)
    return jnp.clip(values, -bound, bound).astype(kind)


def setup_inputs(seed: int = 0) -> dict:
    key_of = jax.random.split(jax.random.key(seed), 8)
    query_tiles = draw_query_tiles(jax.random.fold_in(key_of[7], 71), 0)
    key_tiles = draw_key_tiles(jax.random.fold_in(key_of[7], 71), 0)
    value_tiles = gaussian(key_of[2], (PS_ALL, PC_ALL, PATCH, D), 1.0, 6.0, ((0, 16), (1, 8)))
    out_grad = gaussian(key_of[3], (PS_ALL, PC_ALL, PATCH, D), 1.0, 6.0, ((0, 16), (1, 8)))
    mix_gain = jnp.clip(jnp.exp(jax.random.uniform(key_of[4], (4, D), jnp.float32, math.log(0.1), math.log(0.8))), 0.1, 0.8)
    partners = draw_partners(jax.random.fold_in(key_of[7], 71), 0)
    counts = draw_counts(jax.random.fold_in(key_of[7], 71), 0)
    return dict(query_tiles=query_tiles, key_tiles=key_tiles, value_tiles=value_tiles, out_grad=out_grad, mix_gain=mix_gain, partners=partners, counts=counts)


NEIGHBOR_STEPS = ((-1, -1), (-1, 0), (-1, 1), (0, -1), (0, 0), (0, 1), (1, -1), (1, 0), (1, 1))

def listed_mask(partners, counts, span_start, chord_start, chord_total):
    grid_shape = partners.shape
    span_pos = span_start + lax.broadcasted_iota(jnp.int32, grid_shape, 0)
    chord_pos = chord_start + lax.broadcasted_iota(jnp.int32, grid_shape, 1)
    live_slot = lax.broadcasted_iota(jnp.int32, grid_shape, 2) < counts[:, :, None]
    span_gap = partners // chord_total - span_pos
    chord_gap = partners % chord_total - chord_pos
    columns = [jnp.any(live_slot & (span_gap == span_step) & (chord_gap == chord_step), axis=-1) for span_step, chord_step in NEIGHBOR_STEPS]
    return jnp.stack(columns, axis=-1).astype(jnp.int32)

def mixed_grad(padded, mix_gain):
    centre = padded[1:-1, 1:-1].astype(jnp.float32)
    summed = centre + mix_gain[0] * padded[:-2, 1:-1] + mix_gain[1] * padded[2:, 1:-1]
    summed = summed + mix_gain[2] * padded[1:-1, :-2] + mix_gain[3] * padded[1:-1, 2:]
    return summed.astype(jnp.bfloat16)

def softmax_terms(scores, log_total, keep_rows):
    inner = jnp.where(keep_rows, scores - log_total[..., None], 0.0)
    return jnp.where(keep_rows, jnp.exp(inner), 0.0)

def rounded(values):
    return lax.optimization_barrier(values.astype(jnp.bfloat16)).astype(jnp.float32)

def pad_grid(tiles):
    widths = [(1, 1), (1, 1)] + [(0, 0)] * (tiles.ndim - 2)
    return jnp.pad(tiles, widths)

def reference(query_tiles, key_tiles, value_tiles, out_grad, mix_gain, partners, counts):
    head_dim = D // HEADS
    scaling = float(head_dim) ** (-0.5)
    listed = listed_mask(partners, counts, 0, 0, PC_ALL)
    grad_tiles = mixed_grad(pad_grid(out_grad), mix_gain)
    key_pad = pad_grid(key_tiles)
    value_pad = pad_grid(value_tiles)
    anchor = jnp.int32(0)

    def one_query(flat_index):
        span_at = flat_index // PC_ALL
        chord_at = flat_index % PC_ALL
        query_rows = lax.dynamic_slice(query_tiles, (span_at, chord_at, anchor, anchor), (1, 1, PATCH, D)).reshape(PATCH, HEADS, head_dim).astype(jnp.float32)
        grad_rows = lax.dynamic_slice(grad_tiles, (span_at, chord_at, anchor, anchor), (1, 1, PATCH, D)).reshape(PATCH, HEADS, head_dim).astype(jnp.float32)
        key_rows = lax.dynamic_slice(key_pad, (span_at, chord_at, anchor, anchor), (3, 3, PATCH, D)).reshape(9, PATCH, HEADS, head_dim).astype(jnp.float32)
        value_rows = lax.dynamic_slice(value_pad, (span_at, chord_at, anchor, anchor), (3, 3, PATCH, D)).reshape(9, PATCH, HEADS, head_dim).astype(jnp.float32)
        keep_rows = lax.dynamic_slice(listed, (span_at, chord_at, anchor), (1, 1, 9)).reshape(9)[:, None, None, None] > 0
        scores = jnp.einsum('qhd,okhd->ohqk', query_rows, key_rows) * scaling
        masked = jnp.where(keep_rows, scores, -jnp.inf)
        row_max = lax.optimization_barrier(jnp.max(masked, axis=(0, 3)))
        log_total = row_max + jnp.log(lax.optimization_barrier(jnp.sum(jnp.exp(masked - row_max[None, :, :, None]), axis=(0, 3))))
        prob_full = softmax_terms(scores, log_total[None], keep_rows)
        prob_half = rounded(prob_full)
        attended = jnp.einsum('ohqk,okhd->qhd', prob_half, value_rows)
        row_delta = lax.optimization_barrier(jnp.sum(grad_rows * attended, axis=-1)).T
        prob_grad = jnp.einsum('qhd,okhd->ohqk', grad_rows, value_rows)
        score_grad = rounded(prob_full * (prob_grad - row_delta[None, :, :, None]))
        query_grad = (scaling * jnp.einsum('ohqk,okhd->qhd', score_grad, key_rows)).astype(jnp.bfloat16).reshape(PATCH, D)
        return (query_grad, log_total, row_delta)
    flat_ids = jnp.arange(PS_ALL * PC_ALL, dtype=jnp.int32)
    query_grad, log_total, row_delta = lax.map(one_query, flat_ids)
    row_stats = jnp.stack([log_total, row_delta], 1).reshape(PS_ALL, PC_ALL, 2, HEADS, PATCH)
    stats_pad = pad_grid(row_stats)
    listed_pad = pad_grid(listed)
    query_pad = pad_grid(query_tiles)
    grad_pad = pad_grid(grad_tiles)

    def one_key(flat_index):
        span_at = flat_index // PC_ALL
        chord_at = flat_index % PC_ALL
        key_rows = lax.dynamic_slice(key_tiles, (span_at, chord_at, anchor, anchor), (1, 1, PATCH, D)).reshape(PATCH, HEADS, head_dim).astype(jnp.float32)
        value_rows = lax.dynamic_slice(value_tiles, (span_at, chord_at, anchor, anchor), (1, 1, PATCH, D)).reshape(PATCH, HEADS, head_dim).astype(jnp.float32)
        query_rows = lax.dynamic_slice(query_pad, (span_at, chord_at, anchor, anchor), (3, 3, PATCH, D)).reshape(9, PATCH, HEADS, head_dim).astype(jnp.float32)
        grad_rows = lax.dynamic_slice(grad_pad, (span_at, chord_at, anchor, anchor), (3, 3, PATCH, D)).reshape(9, PATCH, HEADS, head_dim).astype(jnp.float32)
        near_stats = lax.dynamic_slice(stats_pad, (span_at, chord_at, anchor, anchor, anchor), (3, 3, 2, HEADS, PATCH)).reshape(9, 2, HEADS, PATCH)
        pair_table = lax.dynamic_slice(listed_pad, (span_at, chord_at, anchor), (3, 3, 9)).reshape(9, 9)
        keep_rows = jnp.diagonal(jnp.flip(pair_table, axis=1))[:, None, None, None] > 0
        scores = jnp.einsum('oqhd,khd->ohqk', query_rows, key_rows) * scaling
        prob_full = softmax_terms(scores, near_stats[:, 0], keep_rows)
        prob_half = rounded(prob_full)
        prob_grad = jnp.einsum('oqhd,khd->ohqk', grad_rows, value_rows)
        score_grad = rounded(prob_full * (prob_grad - near_stats[:, 1][..., None]))
        key_grad = (scaling * jnp.einsum('ohqk,oqhd->khd', score_grad, query_rows)).astype(jnp.bfloat16).reshape(PATCH, D)
        value_grad = jnp.einsum('ohqk,oqhd->khd', prob_half, grad_rows).astype(jnp.bfloat16).reshape(PATCH, D)
        return (key_grad, value_grad)
    key_grad, value_grad = lax.map(one_key, flat_ids)
    grid = (PS_ALL, PC_ALL, PATCH, D)
    return (query_grad.reshape(grid), key_grad.reshape(grid), value_grad.reshape(grid))
```

```python
import functools

import jax
import jax.numpy as jnp
from jax import lax
from jax.experimental import pallas as pl
from jax.experimental.pallas import tpu as pltpu
from jax.sharding import PartitionSpec as P

PATCH = 128
D = 512
PAIRS = 4
SCALING = 0.125
LOW_FILL = -1e30
NT = (((1,), (1,)), ((), ()))

OWN = (5, 6, 9, 10)
UP, DOWN, LEFT, RIGHT = (1, 2), (13, 14), (4, 8), (7, 11)
CORNERS = (0, 3, 12, 15)


def shifted(x, span_step, chord_step):
    span, chord = lax.axis_size("span"), lax.axis_size("chord")
    pairs = [
        (s * chord + c, ((s + span_step) % span) * chord + (c + chord_step) % chord)
        for s in range(span)
        for c in range(chord)
    ]
    return lax.ppermute(x, ("span", "chord"), pairs)


def stacked_pair(rows):
    lane = lax.broadcasted_iota(jnp.int32, rows.shape, 1)
    zero = jnp.zeros_like(rows)
    return jnp.concatenate(
        [jnp.where(lane < 64, rows, zero), jnp.where(lane >= 64, rows, zero)], axis=0
    )


def cols(h):
    return pl.ds(pl.multiple_of(h * 128, 128), 128)


def product(rows, pair):
    return lax.dot_general(rows, pair, NT, preferred_element_type=jnp.float32)


def matmul(a, b):
    return jnp.dot(a, b, preferred_element_type=jnp.float32)


def diagonal(x):
    return jnp.concatenate([x[:64, :128], x[64:, 128:]], axis=0)


def per_head(row):
    return jnp.concatenate(
        [jnp.broadcast_to(row[:, :128], (64, 128)), jnp.broadcast_to(row[:, 128:], (64, 128))], axis=0
    )


def penalty(listed, p, w):
    return jnp.where(listed[p * 16 + w] > 0, 0.0, -LOW_FILL)


def exponents(s, row, penalties):
    return jnp.concatenate(
        [jnp.exp(s[128 * i : 128 * (i + 1)] - (row + x)) for i, x in enumerate(penalties)], axis=0
    )


def highest(s, penalties):
    tops = [
        jnp.max(s[128 * i : 128 * (i + 1)], axis=0, keepdims=True) - x for i, x in enumerate(penalties)
    ]
    return functools.reduce(jnp.maximum, tops)


def merged(groups, stats, attended):
    tops = [highest(s, penalties) for s, penalties, _ in groups]
    if stats is not None:
        tops.append(stats[0])
    top = functools.reduce(jnp.maximum, tops)
    total, turned = 0.0, 0.0
    for s, penalties, value_turned in groups:
        e = exponents(s, top, penalties)
        total = total + jnp.sum(e, axis=0, keepdims=True)
        turned = turned + matmul(value_turned, e.astype(jnp.bfloat16))
    turned = diagonal(turned)
    if stats is not None:
        fade = jnp.exp(stats[0] - top)
        total = total + stats[1] * fade
        turned = turned + attended * per_head(fade)
    return top, total, turned


def own_totals_kernel(listed, query, key, value, query_pairs, stats_out, attended_out):
    def step(h, carry):
        value_turned = value[:, cols(h)].T
        for p in range(4):
            pair = stacked_pair(query[p, :, cols(h)] * jnp.bfloat16(SCALING))
            query_pairs[h, p] = pair
            groups = []
            for n in range(2):
                rows = slice(256 * n, 256 * (n + 1))
                groups.append(
                    (
                        product(key[rows, cols(h)], pair),
                        [penalty(listed, p, w) for w in OWN[2 * n : 2 * n + 2]],
                        value_turned[:, rows],
                    )
                )
            top, total, turned = merged(groups, None, None)
            stats_out[h, p : p + 1, :] = top
            stats_out[h, 4 + p : 5 + p, :] = total
            attended_out[h, p] = turned
        return carry

    lax.fori_loop(0, PAIRS, step, 0)


def edge_totals_kernel(
    listed, gain, grad, query_pairs, stats_in, attended_in, from_up, from_down, from_left, from_right,
    grad_pairs, grad_turned, stats_out, attended_out,
):
    ends = ((from_up, UP), (from_down, DOWN))
    sides = ((from_left, LEFT), (from_right, RIGHT))

    def step(h, carry):
        def turned(source):
            return source[1, :, :, cols(h)].reshape(256, 128).T

        values = {id(source): turned(source) for source, _ in ends + sides}
        for p in range(4):
            s, c = p // 2, p % 2
            near = (
                grad[0, c, :, cols(h)] if s == 1 else from_up[2, c, :, cols(h)],
                grad[1, c, :, cols(h)] if s == 0 else from_down[2, c, :, cols(h)],
                grad[s, 0, :, cols(h)] if c == 1 else from_left[2, s, :, cols(h)],
                grad[s, 1, :, cols(h)] if c == 0 else from_right[2, s, :, cols(h)],
            )
            own = (s == 1, s == 0, c == 1, c == 0)
            mixed = grad[s, c, :, cols(h)].astype(jnp.float32)
            for n in range(4):
                row = n if own[n] else n + 4
                mixed = mixed + gain[row : row + 1, cols(h)] * near[n].astype(jnp.float32)
            mixed = mixed.astype(jnp.bfloat16)
            grad_pairs[h, p] = stacked_pair(mixed)
            grad_turned[h, p] = mixed.T
            groups = []
            for source, places in (ends[s], sides[c]):
                groups.append(
                    (
                        product(source[0, :, :, cols(h)].reshape(256, 128), query_pairs[h, p]),
                        [penalty(listed, p, w) for w in places],
                        values[id(source)],
                    )
                )
            stats = stats_in[h, p : p + 1, :], stats_in[h, 4 + p : 5 + p, :]
            top, total, attended = merged(groups, stats, attended_in[h, p])
            stats_out[h, p : p + 1, :] = top
            stats_out[h, 4 + p : 5 + p, :] = total
            attended_out[h, p] = attended
        return carry

    lax.fori_loop(0, PAIRS, step, 0)


def gradients(s, g, penalties, log_total, delta):
    prob = exponents(s, log_total, penalties)
    return prob.astype(jnp.bfloat16), (prob * (g - delta)).astype(jnp.bfloat16)


def corner_kernel(
    listed, stats_in, attended_in, query_pairs, grad_pairs, grad_turned, corner_left, corner_right,
    finals, left_back, right_back, dq_out,
):
    patches = range(4)

    def source(p):
        return (corner_left, corner_right)[p % 2]

    def step(h, carry):
        key_rows = [source(p)[0, p // 2, :, cols(h)] for p in patches]
        value_rows = [source(p)[1, p // 2, :, cols(h)] for p in patches]
        scores = [product(key_rows[p], query_pairs[h, p]) for p in patches]
        g = [product(value_rows[p], grad_pairs[h, p]) for p in patches]
        value_turned = [x.T for x in value_rows]
        key_turned = [x.T for x in key_rows]
        half, score_grad = [], []
        for p in patches:
            missing = penalty(listed, p, CORNERS[p])
            old_top, old_total = stats_in[h, p : p + 1, :], stats_in[h, 4 + p : 5 + p, :]
            top = jnp.maximum(old_top, jnp.max(scores[p], axis=0, keepdims=True) - missing)
            fade = jnp.exp(old_top - top)
            e = jnp.exp(scores[p] - (top + missing))
            total = old_total * fade + jnp.sum(e, axis=0, keepdims=True)
            attended = diagonal(matmul(value_turned[p], e.astype(jnp.bfloat16)))
            attended = attended + attended_in[h, p] * per_head(fade)
            dots = grad_turned[h, p].astype(jnp.float32) * attended
            dot = jnp.concatenate(
                [jnp.sum(dots[:64], axis=0, keepdims=True), jnp.sum(dots[64:], axis=0, keepdims=True)], axis=1
            )
            scale = 1.0 / total
            delta = dot * scale
            finals[h, p : p + 1, :] = top + jnp.log(total)
            finals[h, 4 + p : 5 + p, :] = delta
            prob = e * scale
            half.append(prob.astype(jnp.bfloat16))
            score_grad.append((prob * (g[p] - delta)).astype(jnp.bfloat16))
        for p in patches:
            back = (left_back, right_back)[p % 2]
            back[0, p // 2, :, cols(h)] = matmul(score_grad[p], query_pairs[h, p]).astype(jnp.bfloat16)
            back[1, p // 2, :, cols(h)] = matmul(half[p], grad_pairs[h, p]).astype(jnp.bfloat16)
            dq_out[h, p] = diagonal(matmul(key_turned[p], score_grad[p]))
        return carry

    lax.fori_loop(0, PAIRS, step, 0)


def patch_gradients(h, p, key_rows, value_rows, key_turned, listed, places, finals, query_pairs, grad_pairs):
    half, score_grad = gradients(
        product(key_rows, query_pairs[h, p]),
        product(value_rows, grad_pairs[h, p]),
        [penalty(listed, p, w) for w in places],
        finals[h, p : p + 1, :],
        finals[h, 4 + p : 5 + p, :],
    )
    dk = matmul(score_grad, query_pairs[h, p])
    dv = matmul(half, grad_pairs[h, p])
    return dk, dv, diagonal(matmul(key_turned, score_grad))


def edge_kernel(
    listed, finals, query_pairs, grad_pairs, dq_in, from_up, from_down, from_left, from_right,
    up_sum, down_sum, left_back, right_back, dq_out,
):
    ends = ((from_up, UP), (from_down, DOWN))
    sides = ((from_left, LEFT), (from_right, RIGHT))

    def step(h, carry):
        def rows(source, n):
            return source[n, :, :, cols(h)].reshape(256, 128)

        end_sums, side_sums = [0.0, 0.0], [0.0, 0.0]
        for p in range(4):
            s, c = p // 2, p % 2
            pair = ends[s], sides[c]
            key_rows = jnp.concatenate([rows(source, 0) for source, _ in pair], axis=0)
            value_rows = jnp.concatenate([rows(source, 1) for source, _ in pair], axis=0)
            dk, dv, dq = patch_gradients(
                h, p, key_rows, value_rows, key_rows.T, listed, pair[0][1] + pair[1][1],
                finals, query_pairs, grad_pairs,
            )
            dq_out[h, p] = dq_in[h, p] + dq
            both = jnp.concatenate([dk, dv], axis=1)
            end_sums[s] = end_sums[s] + both[:256]
            side_sums[c] = side_sums[c] + both[256:]
        for s, back in enumerate((up_sum, down_sum)):
            for at in range(2):
                for n in range(2):
                    back[n, at, :, cols(h)] = end_sums[s][128 * at : 128 * (at + 1), 128 * n : 128 * (n + 1)]
        for c, back in enumerate((left_back, right_back)):
            for at in range(2):
                for n in range(2):
                    part = side_sums[c][128 * at : 128 * (at + 1), 128 * n : 128 * (n + 1)]
                    back[n, at, :, cols(h)] = part.astype(jnp.bfloat16)
        return carry

    lax.fori_loop(0, PAIRS, step, 0)


def add_kernel(listed, up_sum, down_sum, add_left, add_right, up_back, down_back):
    for n in range(2):
        for s, (total, back) in enumerate(((up_sum, up_back), (down_sum, down_back))):
            for at, added in enumerate((add_left, add_right)):
                back[n, at] = (total[n, at] + added[n, s].astype(jnp.float32)).astype(jnp.bfloat16)


def last_kernel(listed, own_key, own_value, left, right, up, down, key_grad, value_grad):
    for n, (own, out) in enumerate(((own_key, key_grad), (own_value, value_grad))):
        for p in range(4):
            s, c = p // 2, p % 2
            beside = (left, right)[c][n, s].astype(jnp.float32)
            end = (up, down)[s][n, c].astype(jnp.float32)
            total = own[128 * p : 128 * (p + 1), :] + beside + end
            out[s, c] = total.astype(jnp.bfloat16)


def own_kernel(
    listed, finals, query_pairs, grad_pairs, key, value, dq_in, own_key, own_value, query_grad
):
    def step(h, carry):
        key_rows, value_rows = key[:, cols(h)], value[:, cols(h)]
        key_turned = key_rows.T
        dk, dv = 0.0, 0.0
        for p in range(4):
            more_dk, more_dv, dq = patch_gradients(
                h, p, key_rows, value_rows, key_turned, listed, OWN, finals, query_pairs, grad_pairs
            )
            dk, dv = dk + more_dk, dv + more_dv
            query_grad[p, :, cols(h)] = (SCALING * (dq_in[h, p] + dq).T).astype(jnp.bfloat16)
        own_key[:, cols(h)] = dk
        own_value[:, cols(h)] = dv
        return carry

    lax.fori_loop(0, PAIRS, step, 0)


BF16, F32 = jnp.bfloat16, jnp.float32
TILE = (PATCH, D)
IN_VMEM = pl.BlockSpec(memory_space=pltpu.VMEM)
IN_SMEM = pl.BlockSpec(memory_space=pltpu.SMEM)


def call(kernel, outs, flops, listed, *args):
    return pl.pallas_call(
        kernel,
        out_shape=[jax.ShapeDtypeStruct(shape, kind) for shape, kind in outs],
        in_specs=[IN_SMEM] + [IN_VMEM] * len(args),
        out_specs=[IN_VMEM] * len(outs),
        compiler_params=pltpu.CompilerParams(vmem_limit_bytes=40 * 1024 * 1024),
        cost_estimate=pl.CostEstimate(flops=flops, bytes_accessed=10**6, transcendentals=0),
    )(listed, *args)


PAIR_SHAPE = ((PAIRS, 4, 256, 128), BF16)
TURNED = ((PAIRS, 4, 128, PATCH), F32)
STATS = ((PAIRS, 8, 256), F32)
TWO = ((2, 2) + TILE, BF16)


def local(query_tiles, key_tiles, value_tiles, out_grad, mix_gain, partners, counts):
    span_at, chord_at = lax.axis_index("span"), lax.axis_index("chord")
    span_end, chord_end = lax.axis_size("span") - 1, lax.axis_size("chord") - 1
    chord_total = 2 * lax.axis_size("chord")
    span_pos = partners // chord_total - 2 * span_at + 1
    chord_pos = partners % chord_total - 2 * chord_at + 1
    slots = (span_pos * 4 + chord_pos).reshape(4, 8, 1)
    live = lax.broadcasted_iota(jnp.int32, (4, 8, 16), 1) < counts.reshape(4, 1, 1)
    matches = slots == lax.broadcasted_iota(jnp.int32, (4, 8, 16), 2)
    listed = jnp.any(live & matches, axis=1).astype(jnp.int32).reshape(64)
    inside = jnp.stack([span_at > 0, span_at < span_end, chord_at > 0, chord_at < chord_end])
    gain = jnp.concatenate([mix_gain, jnp.where(inside[:, None], mix_gain, 0.0)], axis=0)

    def packed(*index):
        return jnp.stack([x[index] for x in (key_tiles, value_tiles, out_grad)])

    every = slice(None)
    from_up = shifted(packed(1), 1, 0)
    from_down = shifted(packed(0), -1, 0)
    from_left = shifted(packed(every, 1), 0, 1)
    from_right = shifted(packed(every, 0), 0, -1)

    def corners(c):
        return jnp.stack([from_up[:2, c], from_down[:2, c]], axis=1)

    corner_left = shifted(corners(1), 0, 1)
    corner_right = shifted(corners(0), 0, -1)

    key_rows, value_rows = key_tiles.reshape(4 * PATCH, D), value_tiles.reshape(4 * PATCH, D)
    query_pairs, stats, attended = call(
        own_totals_kernel, [PAIR_SHAPE, STATS, TURNED], 6 * 10**9,
        listed, query_tiles.reshape((4,) + TILE), key_rows, value_rows,
    )
    grad_pairs, grad_turned, stats, attended = call(
        edge_totals_kernel, [PAIR_SHAPE, ((PAIRS, 4, 128, PATCH), BF16), STATS, TURNED], 6 * 10**9,
        listed, gain, out_grad, query_pairs, stats, attended, from_up, from_down, from_left, from_right,
    )
    pairs = query_pairs, grad_pairs
    finals, left_back, right_back, dq = call(
        corner_kernel, [STATS, TWO, TWO, TURNED], 2 * 10**9,
        listed, stats, attended, *pairs, grad_turned, corner_left, corner_right,
    )
    add_right = shifted(left_back, 0, -1)
    add_left = shifted(right_back, 0, 1)
    wide = ((2, 2) + TILE, F32)
    up_sum, down_sum, left_back, right_back, dq = call(
        edge_kernel, [wide, wide, TWO, TWO, TURNED], 8 * 10**9,
        listed, finals, *pairs, dq, from_up, from_down, from_left, from_right,
    )
    up_back, down_back = call(
        add_kernel, [TWO, TWO], 10**7, listed, up_sum, down_sum, add_left, add_right
    )
    end_down = shifted(up_back, -1, 0)
    end_up = shifted(down_back, 1, 0)
    side_right = shifted(left_back, 0, -1)
    side_left = shifted(right_back, 0, 1)
    own_key, own_value, query_grad = call(
        own_kernel, [((4 * PATCH, D), F32), ((4 * PATCH, D), F32), ((4,) + TILE, BF16)], 10**10,
        listed, finals, *pairs, key_rows, value_rows, dq,
    )

    key_grad, value_grad = call(
        last_kernel, [TWO, TWO], 10**7,
        listed, own_key, own_value, side_left, side_right, end_up, end_down,
    )
    return (query_grad.reshape((2, 2) + TILE), key_grad, value_grad)


def solution(mesh):
    tiles = P("span", "chord", None, None)
    in_specs = (tiles, tiles, tiles, tiles, P(), P("span", "chord", None), P("span", "chord"))
    return jax.shard_map(
        local, mesh=mesh, in_specs=in_specs, out_specs=(tiles, tiles, tiles), check_vma=False
    )
```

```python
import functools

import jax
import jax.numpy as jnp
from jax import lax
from jax.experimental import pallas as pl
from jax.experimental.pallas import tpu as pltpu
from jax.sharding import PartitionSpec as P

PATCH = 128
D = 512
PAIRS = 4
SCALING = 0.125
LOW_FILL = -1e30
NT = (((1,), (1,)), ((), ()))

OWN = (5, 6, 9, 10)
UP, DOWN, LEFT, RIGHT = (1, 2), (13, 14), (4, 8), (7, 11)
CORNERS = (0, 3, 12, 15)


def shifted(x, span_step, chord_step):
    span, chord = lax.axis_size("span"), lax.axis_size("chord")
    pairs = [
        (s * chord + c, ((s + span_step) % span) * chord + (c + chord_step) % chord)
        for s in range(span)
        for c in range(chord)
    ]
    return lax.ppermute(x, ("span", "chord"), pairs)


def stacked_pair(rows):
    lane = lax.broadcasted_iota(jnp.int32, rows.shape, 1)
    zero = jnp.zeros_like(rows)
    return jnp.concatenate(
        [jnp.where(lane < 64, rows, zero), jnp.where(lane >= 64, rows, zero)], axis=0
    )


def cols(h):
    return pl.ds(pl.multiple_of(h * 128, 128), 128)


def product(rows, pair):
    return lax.dot_general(rows, pair, NT, preferred_element_type=jnp.float32)


def matmul(a, b):
    return jnp.dot(a, b, preferred_element_type=jnp.float32)


def diagonal(x):
    return jnp.concatenate([x[:64, :128], x[64:, 128:]], axis=0)


def per_head(row):
    return jnp.concatenate(
        [jnp.broadcast_to(row[:, :128], (64, 128)), jnp.broadcast_to(row[:, 128:], (64, 128))], axis=0
    )


def penalty(listed, p, w):
    return jnp.where(listed[p * 16 + w] > 0, 0.0, -LOW_FILL)


def exponents(s, row, penalties):
    return jnp.concatenate(
        [jnp.exp(s[128 * i : 128 * (i + 1)] - (row + x)) for i, x in enumerate(penalties)], axis=0
    )


def highest(s, penalties):
    tops = [
        jnp.max(s[128 * i : 128 * (i + 1)], axis=0, keepdims=True) - x for i, x in enumerate(penalties)
    ]
    return functools.reduce(jnp.maximum, tops)


def merged(groups, stats, attended):
    tops = [highest(s, penalties) for s, penalties, _ in groups]
    if stats is not None:
        tops.append(stats[0])
    top = functools.reduce(jnp.maximum, tops)
    total, turned = 0.0, 0.0
    for s, penalties, value_turned in groups:
        e = exponents(s, top, penalties)
        total = total + jnp.sum(e, axis=0, keepdims=True)
        turned = turned + matmul(value_turned, e.astype(jnp.bfloat16))
    turned = diagonal(turned)
    if stats is not None:
        fade = jnp.exp(stats[0] - top)
        total = total + stats[1] * fade
        turned = turned + attended * per_head(fade)
    return top, total, turned


def own_totals_kernel(
    chord_total, partners, counts, query, key, value, listed, query_pairs, stats_out, attended_out
):
    for i in range(72):
        listed[i] = 0
    for p in range(4):
        s, c = p // 2, p % 2
        own = partners[s, c, 0]
        for j in range(8):
            other = partners[s, c, j]
            row = 1 + s + lax.div(other, chord_total) - lax.div(own, chord_total)
            column = 1 + c + lax.rem(other, chord_total) - lax.rem(own, chord_total)
            listed[jnp.where(j < counts[s, c], p * 16 + row * 4 + column, 64)] = 1

    def step(h, carry):
        value_turned = value[:, cols(h)].T
        for p in range(4):
            pair = stacked_pair(query[p, :, cols(h)] * jnp.bfloat16(SCALING))
            query_pairs[h, p] = pair
            groups = []
            for n in range(2):
                rows = slice(256 * n, 256 * (n + 1))
                groups.append(
                    (
                        product(key[rows, cols(h)], pair),
                        [penalty(listed, p, w) for w in OWN[2 * n : 2 * n + 2]],
                        value_turned[:, rows],
                    )
                )
            top, total, turned = merged(groups, None, None)
            stats_out[h, p : p + 1, :] = top
            stats_out[h, 4 + p : 5 + p, :] = total
            attended_out[h, p] = turned
        return carry

    lax.fori_loop(0, PAIRS, step, 0)


def edge_totals_kernel(
    listed, query_pairs, stats_in, attended_in, from_up, from_down, from_left, from_right,
    stats_out, attended_out,
):
    ends = ((from_up, UP), (from_down, DOWN))
    sides = ((from_left, LEFT), (from_right, RIGHT))

    def step(h, carry):
        def turned(source):
            return source[1, :, :, cols(h)].reshape(256, 128).T

        values = {id(source): turned(source) for source, _ in ends + sides}
        for p in range(4):
            s, c = p // 2, p % 2
            groups = []
            for source, places in (ends[s], sides[c]):
                groups.append(
                    (
                        product(source[0, :, :, cols(h)].reshape(256, 128), query_pairs[h, p]),
                        [penalty(listed, p, w) for w in places],
                        values[id(source)],
                    )
                )
            stats = stats_in[h, p : p + 1, :], stats_in[h, 4 + p : 5 + p, :]
            top, total, attended = merged(groups, stats, attended_in[h, p])
            stats_out[h, p : p + 1, :] = top
            stats_out[h, 4 + p : 5 + p, :] = total
            attended_out[h, p] = attended
        return carry

    lax.fori_loop(0, PAIRS, step, 0)


def gradients(s, g, penalties, log_total, delta):
    prob = exponents(s, log_total, penalties)
    return prob.astype(jnp.bfloat16), (prob * (g - delta)).astype(jnp.bfloat16)


def corner_kernel(
    span_total, chord_total, listed, partners, gain, grad, grad_up, grad_down, from_left, from_right,
    stats_in, attended_in, query_pairs, corner_left, corner_right,
    grad_pairs, finals, left_back, right_back, dq_out,
):
    first = partners[0, 0, 0]
    row, column = lax.div(first, chord_total), lax.rem(first, chord_total)
    inside = [
        jnp.where(x, 1.0, 0.0)
        for x in (row > 0, row < span_total - 2, column > 0, column < chord_total - 2)
    ]
    patches = range(4)

    def source(p):
        return (corner_left, corner_right)[p % 2]

    def step(h, carry):
        pairs, grad_turned = [], []
        for p in patches:
            s, c = p // 2, p % 2
            near = (
                grad[0, c, :, cols(h)] if s == 1 else grad_up[c, :, cols(h)],
                grad[1, c, :, cols(h)] if s == 0 else grad_down[c, :, cols(h)],
                grad[s, 0, :, cols(h)] if c == 1 else from_left[2, s, :, cols(h)],
                grad[s, 1, :, cols(h)] if c == 0 else from_right[2, s, :, cols(h)],
            )
            own = (s == 1, s == 0, c == 1, c == 0)
            mixed = grad[s, c, :, cols(h)].astype(jnp.float32)
            for n in range(4):
                factor = gain[n : n + 1, cols(h)]
                if not own[n]:
                    factor = factor * inside[n]
                mixed = mixed + factor * near[n].astype(jnp.float32)
            mixed = mixed.astype(jnp.bfloat16)
            pair = stacked_pair(mixed)
            grad_pairs[h, p] = pair
            pairs.append(pair)
            grad_turned.append(mixed.T)
        key_rows = [source(p)[0, p // 2, :, cols(h)] for p in patches]
        value_rows = [source(p)[1, p // 2, :, cols(h)] for p in patches]
        scores = [product(key_rows[p], query_pairs[h, p]) for p in patches]
        g = [product(value_rows[p], pairs[p]) for p in patches]
        value_turned = [x.T for x in value_rows]
        key_turned = [x.T for x in key_rows]
        half, score_grad = [], []
        for p in patches:
            missing = penalty(listed, p, CORNERS[p])
            old_top, old_total = stats_in[h, p : p + 1, :], stats_in[h, 4 + p : 5 + p, :]
            top = jnp.maximum(old_top, jnp.max(scores[p], axis=0, keepdims=True) - missing)
            fade = jnp.exp(old_top - top)
            e = jnp.exp(scores[p] - (top + missing))
            total = old_total * fade + jnp.sum(e, axis=0, keepdims=True)
            attended = diagonal(matmul(value_turned[p], e.astype(jnp.bfloat16)))
            attended = attended + attended_in[h, p] * per_head(fade)
            dots = grad_turned[p].astype(jnp.float32) * attended
            dot = jnp.concatenate(
                [jnp.sum(dots[:64], axis=0, keepdims=True), jnp.sum(dots[64:], axis=0, keepdims=True)], axis=1
            )
            scale = 1.0 / total
            delta = dot * scale
            finals[h, p : p + 1, :] = top + jnp.log(total)
            finals[h, 4 + p : 5 + p, :] = delta
            prob = e * scale
            half.append(prob.astype(jnp.bfloat16))
            score_grad.append((prob * (g[p] - delta)).astype(jnp.bfloat16))
        for p in patches:
            back = (left_back, right_back)[p % 2]
            back[0, p // 2, :, cols(h)] = matmul(score_grad[p], query_pairs[h, p]).astype(jnp.bfloat16)
            back[1, p // 2, :, cols(h)] = matmul(half[p], pairs[p]).astype(jnp.bfloat16)
            dq_out[h, p] = diagonal(matmul(key_turned[p], score_grad[p]))
        return carry

    lax.fori_loop(0, PAIRS, step, 0)


def patch_gradients(h, p, key_rows, value_rows, key_turned, listed, places, finals, query_pairs, grad_pairs):
    half, score_grad = gradients(
        product(key_rows, query_pairs[h, p]),
        product(value_rows, grad_pairs[h, p]),
        [penalty(listed, p, w) for w in places],
        finals[h, p : p + 1, :],
        finals[h, 4 + p : 5 + p, :],
    )
    dk = matmul(score_grad, query_pairs[h, p])
    dv = matmul(half, grad_pairs[h, p])
    return dk, dv, diagonal(matmul(key_turned, score_grad))


def edge_kernel(
    listed, finals, query_pairs, grad_pairs, dq_in, from_up, from_down, from_left, from_right,
    up_sum, down_sum, left_back, right_back, dq_out,
):
    ends = ((from_up, UP), (from_down, DOWN))
    sides = ((from_left, LEFT), (from_right, RIGHT))

    def step(h, carry):
        def rows(source, n):
            return source[n, :, :, cols(h)].reshape(256, 128)

        end_sums, side_sums = [0.0, 0.0], [0.0, 0.0]
        for p in range(4):
            s, c = p // 2, p % 2
            pair = ends[s], sides[c]
            key_rows = jnp.concatenate([rows(source, 0) for source, _ in pair], axis=0)
            value_rows = jnp.concatenate([rows(source, 1) for source, _ in pair], axis=0)
            dk, dv, dq = patch_gradients(
                h, p, key_rows, value_rows, key_rows.T, listed, pair[0][1] + pair[1][1],
                finals, query_pairs, grad_pairs,
            )
            dq_out[h, p] = dq_in[h, p] + dq
            both = jnp.concatenate([dk, dv], axis=1)
            end_sums[s] = end_sums[s] + both[:256]
            side_sums[c] = side_sums[c] + both[256:]
        for s, back in enumerate((up_sum, down_sum)):
            for at in range(2):
                for n in range(2):
                    back[n, at, :, cols(h)] = end_sums[s][128 * at : 128 * (at + 1), 128 * n : 128 * (n + 1)]
        for c, back in enumerate((left_back, right_back)):
            for at in range(2):
                for n in range(2):
                    part = side_sums[c][128 * at : 128 * (at + 1), 128 * n : 128 * (n + 1)]
                    back[n, at, :, cols(h)] = part.astype(jnp.bfloat16)
        return carry

    lax.fori_loop(0, PAIRS, step, 0)


def add_kernel(up_sum, down_sum, add_left, add_right, up_back, down_back):
    for n in range(2):
        for s, (total, back) in enumerate(((up_sum, up_back), (down_sum, down_back))):
            for at, added in enumerate((add_left, add_right)):
                back[n, at] = (total[n, at] + added[n, s].astype(jnp.float32)).astype(jnp.bfloat16)


def last_kernel(own_key, own_value, left, right, up, down, key_grad, value_grad):
    for n, (own, out) in enumerate(((own_key, key_grad), (own_value, value_grad))):
        for p in range(4):
            s, c = p // 2, p % 2
            beside = (left, right)[c][n, s].astype(jnp.float32)
            end = (up, down)[s][n, c].astype(jnp.float32)
            total = own[128 * p : 128 * (p + 1), :] + beside + end
            out[s, c] = total.astype(jnp.bfloat16)


def own_kernel(
    listed, finals, query_pairs, grad_pairs, key, value, dq_in, own_key, own_value, query_grad
):
    def step(h, carry):
        key_rows, value_rows = key[:, cols(h)], value[:, cols(h)]
        key_turned = key_rows.T
        joined_query = jnp.concatenate([query_pairs[h, p] for p in range(4)], axis=0)
        joined_grad = jnp.concatenate([grad_pairs[h, p] for p in range(4)], axis=0)
        terms = [
            gradients(
                product(key_rows, query_pairs[h, p]),
                product(value_rows, grad_pairs[h, p]),
                [penalty(listed, p, w) for w in OWN],
                finals[h, p : p + 1, :],
                finals[h, 4 + p : 5 + p, :],
            )
            for p in range(4)
        ]
        dq = [diagonal(matmul(key_turned, score_grad)) for _, score_grad in terms]
        dk = matmul(jnp.concatenate([score_grad for _, score_grad in terms], axis=1), joined_query)
        dv = matmul(jnp.concatenate([half for half, _ in terms], axis=1), joined_grad)
        for p in range(4):
            query_grad[p, :, cols(h)] = (SCALING * (dq_in[h, p] + dq[p]).T).astype(jnp.bfloat16)
        own_key[:, cols(h)] = dk
        own_value[:, cols(h)] = dv
        return carry

    lax.fori_loop(0, PAIRS, step, 0)


BF16, F32 = jnp.bfloat16, jnp.float32
TILE = (PATCH, D)
IN_VMEM = pl.BlockSpec(memory_space=pltpu.VMEM)
IN_SMEM = pl.BlockSpec(memory_space=pltpu.SMEM)


def call(kernel, outs, flops, *args):
    def space(kind):
        return IN_SMEM if kind == jnp.int32 else IN_VMEM

    return pl.pallas_call(
        kernel,
        out_shape=[jax.ShapeDtypeStruct(shape, kind) for shape, kind in outs],
        in_specs=[space(x.dtype) for x in args],
        out_specs=[space(kind) for _, kind in outs],
        compiler_params=pltpu.CompilerParams(vmem_limit_bytes=40 * 1024 * 1024),
        cost_estimate=pl.CostEstimate(flops=flops, bytes_accessed=10**6, transcendentals=0),
    )(*args)


PAIR_SHAPE = ((PAIRS, 4, 256, 128), BF16)
TURNED = ((PAIRS, 4, 128, PATCH), F32)
STATS = ((PAIRS, 8, 256), F32)
TWO = ((2, 2) + TILE, BF16)


def local(query_tiles, key_tiles, value_tiles, out_grad, mix_gain, partners, counts):
    span_total, chord_total = 2 * lax.axis_size("span"), 2 * lax.axis_size("chord")
    every = slice(None)

    def packed(tiles, *index):
        return jnp.stack([x[index] for x in tiles])

    from_up = shifted(packed((key_tiles, value_tiles), 1), 1, 0)
    from_down = shifted(packed((key_tiles, value_tiles), 0), -1, 0)
    from_left = shifted(packed((key_tiles, value_tiles, out_grad), every, 1), 0, 1)
    from_right = shifted(packed((key_tiles, value_tiles, out_grad), every, 0), 0, -1)

    def corners(c):
        return jnp.stack([from_up[:, c], from_down[:, c]], axis=1)

    corner_left = shifted(corners(1), 0, 1)
    corner_right = shifted(corners(0), 0, -1)

    key_rows, value_rows = key_tiles.reshape(4 * PATCH, D), value_tiles.reshape(4 * PATCH, D)
    listed, query_pairs, stats, attended = call(
        functools.partial(own_totals_kernel, chord_total),
        [((72,), jnp.int32), PAIR_SHAPE, STATS, TURNED], 6 * 10**9,
        partners, counts, query_tiles.reshape((4,) + TILE), key_rows, value_rows,
    )
    upper, lower, stats = lax.optimization_barrier((out_grad[0], out_grad[1], stats))
    grad_up, grad_down = shifted(lower, 1, 0), shifted(upper, -1, 0)
    stats, attended = call(
        edge_totals_kernel, [STATS, TURNED], 6 * 10**9,
        listed, query_pairs, stats, attended, from_up, from_down, from_left, from_right,
    )
    grad_pairs, finals, left_back, right_back, dq = call(
        functools.partial(corner_kernel, span_total, chord_total),
        [PAIR_SHAPE, STATS, TWO, TWO, TURNED], 3 * 10**9,
        listed, partners, mix_gain, out_grad, grad_up, grad_down, from_left, from_right,
        stats, attended, query_pairs, corner_left, corner_right,
    )
    pairs = query_pairs, grad_pairs
    add_right = shifted(left_back, 0, -1)
    add_left = shifted(right_back, 0, 1)
    wide = ((2, 2) + TILE, F32)
    up_sum, down_sum, left_back, right_back, dq = call(
        edge_kernel, [wide, wide, TWO, TWO, TURNED], 8 * 10**9,
        listed, finals, *pairs, dq, from_up, from_down, from_left, from_right,
    )
    up_back, down_back = call(
        add_kernel, [TWO, TWO], 10**7, up_sum, down_sum, add_left, add_right
    )
    end_down = shifted(up_back, -1, 0)
    end_up = shifted(down_back, 1, 0)
    left_back, right_back, *_ = lax.optimization_barrier((left_back, right_back, up_back, down_back))
    side_right = shifted(left_back, 0, -1)
    side_left = shifted(right_back, 0, 1)
    own_key, own_value, query_grad = call(
        own_kernel, [((4 * PATCH, D), F32), ((4 * PATCH, D), F32), ((4,) + TILE, BF16)], 10**10,
        listed, finals, *pairs, key_rows, value_rows, dq,
    )

    key_grad, value_grad = call(
        last_kernel, [TWO, TWO], 10**7,
        own_key, own_value, side_left, side_right, end_up, end_down,
    )
    return (query_grad.reshape((2, 2) + TILE), key_grad, value_grad)


def solution(mesh):
    tiles = P("span", "chord", None, None)
    in_specs = (tiles, tiles, tiles, tiles, P(), P("span", "chord", None), P("span", "chord"))
    return jax.shard_map(
        local, mesh=mesh, in_specs=in_specs, out_specs=(tiles, tiles, tiles), check_vma=False
    )
```

```python
import functools

import jax
import jax.numpy as jnp
from jax import lax
from jax.experimental import pallas as pl
from jax.experimental.pallas import tpu as pltpu
from jax.sharding import PartitionSpec as P

PATCH = 128
D = 512
PAIRS = 4
SCALING = 0.125
LOW_FILL = -1e30
NT = (((1,), (1,)), ((), ()))

OWN = (5, 6, 9, 10)
UP, DOWN, LEFT, RIGHT = (1, 2), (13, 14), (4, 8), (7, 11)
CORNERS = (0, 3, 12, 15)


def shifted(x, span_step, chord_step):
    span, chord = lax.axis_size("span"), lax.axis_size("chord")
    pairs = [
        (s * chord + c, ((s + span_step) % span) * chord + (c + chord_step) % chord)
        for s in range(span)
        for c in range(chord)
    ]
    return lax.ppermute(x, ("span", "chord"), pairs)


def stacked_pair(rows):
    lane = lax.broadcasted_iota(jnp.int32, rows.shape, 1)
    zero = jnp.zeros_like(rows)
    return jnp.concatenate(
        [jnp.where(lane < 64, rows, zero), jnp.where(lane >= 64, rows, zero)], axis=0
    )


def cols(h):
    return pl.ds(pl.multiple_of(h * 128, 128), 128)


def product(rows, pair):
    return lax.dot_general(rows, pair, NT, preferred_element_type=jnp.float32)


def matmul(a, b):
    return jnp.dot(a, b, preferred_element_type=jnp.float32)


def diagonal(x):
    return jnp.concatenate([x[:64, :128], x[64:, 128:]], axis=0)


def per_head(row):
    return jnp.concatenate(
        [jnp.broadcast_to(row[:, :128], (64, 128)), jnp.broadcast_to(row[:, 128:], (64, 128))], axis=0
    )


def penalty(listed, p, w):
    return jnp.where(listed[p * 16 + w] > 0, 0.0, -LOW_FILL)


def exponents(s, row, penalties):
    return jnp.concatenate(
        [jnp.exp(s[128 * i : 128 * (i + 1)] - (row + x)) for i, x in enumerate(penalties)], axis=0
    )


def highest(s, penalties):
    tops = [
        jnp.max(s[128 * i : 128 * (i + 1)], axis=0, keepdims=True) - x for i, x in enumerate(penalties)
    ]
    return functools.reduce(jnp.maximum, tops)


def merged(groups, stats, attended):
    tops = [highest(s, penalties) for s, penalties, _ in groups]
    if stats is not None:
        tops.append(stats[0])
    top = functools.reduce(jnp.maximum, tops)
    total, turned = 0.0, 0.0
    for s, penalties, value_turned in groups:
        e = exponents(s, top, penalties)
        total = total + jnp.sum(e, axis=0, keepdims=True)
        turned = turned + matmul(value_turned, e.astype(jnp.bfloat16))
    turned = diagonal(turned)
    if stats is not None:
        fade = jnp.exp(stats[0] - top)
        total = total + stats[1] * fade
        turned = turned + attended * per_head(fade)
    return top, total, turned


def own_totals_kernel(
    chord_total, partners, counts, query, key, value, listed, query_pairs, stats_out, attended_out
):
    for i in range(72):
        listed[i] = 0
    for p in range(4):
        s, c = p // 2, p % 2
        own = partners[s, c, 0]
        for j in range(8):
            other = partners[s, c, j]
            row = 1 + s + lax.div(other, chord_total) - lax.div(own, chord_total)
            column = 1 + c + lax.rem(other, chord_total) - lax.rem(own, chord_total)
            listed[jnp.where(j < counts[s, c], p * 16 + row * 4 + column, 64)] = 1

    def step(h, carry):
        value_turned = value[:, cols(h)].T

        def groups_of(p):
            pair = stacked_pair(query[p, :, cols(h)] * jnp.bfloat16(SCALING))
            query_pairs[h, p] = pair
            groups = []
            for n in range(2):
                rows = slice(256 * n, 256 * (n + 1))
                groups.append(
                    (
                        product(key[rows, cols(h)], pair),
                        [penalty(listed, p, w) for w in OWN[2 * n : 2 * n + 2]],
                        value_turned[:, rows],
                    )
                )
            return groups

        ahead = groups_of(0)
        for p in range(4):
            groups = ahead
            ahead = groups_of(p + 1) if p < 3 else None
            top, total, turned = merged(groups, None, None)
            stats_out[h, p : p + 1, :] = top
            stats_out[h, 4 + p : 5 + p, :] = total
            attended_out[h, p] = turned
        return carry

    lax.fori_loop(0, PAIRS, step, 0)


def edge_totals_kernel(
    listed, query_pairs, stats_in, attended_in, from_up, from_down, from_left, from_right,
    stats_out, attended_out,
):
    ends = ((from_up, UP), (from_down, DOWN))
    sides = ((from_left, LEFT), (from_right, RIGHT))

    def step(h, carry):
        def turned(source):
            return source[1, :, :, cols(h)].reshape(256, 128).T

        values = {id(source): turned(source) for source, _ in ends + sides}

        def groups_of(p):
            return [
                (
                    product(source[0, :, :, cols(h)].reshape(256, 128), query_pairs[h, p]),
                    [penalty(listed, p, w) for w in places],
                    values[id(source)],
                )
                for source, places in (ends[p // 2], sides[p % 2])
            ]

        ahead = groups_of(0)
        for p in range(4):
            groups = ahead
            ahead = groups_of(p + 1) if p < 3 else None
            stats = stats_in[h, p : p + 1, :], stats_in[h, 4 + p : 5 + p, :]
            top, total, attended = merged(groups, stats, attended_in[h, p])
            stats_out[h, p : p + 1, :] = top
            stats_out[h, 4 + p : 5 + p, :] = total
            attended_out[h, p] = attended
        return carry

    lax.fori_loop(0, PAIRS, step, 0)


def gradients(s, g, penalties, log_total, delta):
    prob = exponents(s, log_total, penalties)
    return prob.astype(jnp.bfloat16), (prob * (g - delta)).astype(jnp.bfloat16)


def corner_kernel(
    span_total, chord_total, listed, partners, gain, grad, grad_up, grad_down, from_left, from_right,
    stats_in, attended_in, query_pairs, corner_left, corner_right,
    grad_pairs, finals, left_back, right_back, dq_out,
):
    first = partners[0, 0, 0]
    row, column = lax.div(first, chord_total), lax.rem(first, chord_total)
    inside = [
        jnp.where(x, 1.0, 0.0)
        for x in (row > 0, row < span_total - 2, column > 0, column < chord_total - 2)
    ]
    patches = range(4)

    def source(p):
        return (corner_left, corner_right)[p % 2]

    def step(h, carry):
        pairs, grad_turned = [], []
        for p in patches:
            s, c = p // 2, p % 2
            near = (
                grad[0, c, :, cols(h)] if s == 1 else grad_up[c, :, cols(h)],
                grad[1, c, :, cols(h)] if s == 0 else grad_down[c, :, cols(h)],
                grad[s, 0, :, cols(h)] if c == 1 else from_left[2, s, :, cols(h)],
                grad[s, 1, :, cols(h)] if c == 0 else from_right[2, s, :, cols(h)],
            )
            own = (s == 1, s == 0, c == 1, c == 0)
            mixed = grad[s, c, :, cols(h)].astype(jnp.float32)
            for n in range(4):
                factor = gain[n : n + 1, cols(h)]
                if not own[n]:
                    factor = factor * inside[n]
                mixed = mixed + factor * near[n].astype(jnp.float32)
            mixed = mixed.astype(jnp.bfloat16)
            pair = stacked_pair(mixed)
            grad_pairs[h, p] = pair
            pairs.append(pair)
            grad_turned.append(mixed.T)
        key_rows = [source(p)[0, p // 2, :, cols(h)] for p in patches]
        value_rows = [source(p)[1, p // 2, :, cols(h)] for p in patches]
        scores = [product(key_rows[p], query_pairs[h, p]) for p in patches]
        g = [product(value_rows[p], pairs[p]) for p in patches]
        value_turned = [x.T for x in value_rows]
        key_turned = [x.T for x in key_rows]
        half, score_grad = [], []
        for p in patches:
            missing = penalty(listed, p, CORNERS[p])
            old_top, old_total = stats_in[h, p : p + 1, :], stats_in[h, 4 + p : 5 + p, :]
            top = jnp.maximum(old_top, jnp.max(scores[p], axis=0, keepdims=True) - missing)
            fade = jnp.exp(old_top - top)
            e = jnp.exp(scores[p] - (top + missing))
            total = old_total * fade + jnp.sum(e, axis=0, keepdims=True)
            attended = diagonal(matmul(value_turned[p], e.astype(jnp.bfloat16)))
            attended = attended + attended_in[h, p] * per_head(fade)
            dots = grad_turned[p].astype(jnp.float32) * attended
            dot = jnp.concatenate(
                [jnp.sum(dots[:64], axis=0, keepdims=True), jnp.sum(dots[64:], axis=0, keepdims=True)], axis=1
            )
            scale = 1.0 / total
            delta = dot * scale
            finals[h, p : p + 1, :] = top + jnp.log(total)
            finals[h, 4 + p : 5 + p, :] = delta
            prob = e * scale
            half.append(prob.astype(jnp.bfloat16))
            score_grad.append((prob * (g[p] - delta)).astype(jnp.bfloat16))
        for p in patches:
            back = (left_back, right_back)[p % 2]
            back[0, p // 2, :, cols(h)] = matmul(score_grad[p], query_pairs[h, p]).astype(jnp.bfloat16)
            back[1, p // 2, :, cols(h)] = matmul(half[p], pairs[p]).astype(jnp.bfloat16)
            dq_out[h, p] = diagonal(matmul(key_turned[p], score_grad[p]))
        return carry

    lax.fori_loop(0, PAIRS, step, 0)


def patch_gradients(h, p, key_rows, value_rows, key_turned, listed, places, finals, query_pairs, grad_pairs):
    half, score_grad = gradients(
        product(key_rows, query_pairs[h, p]),
        product(value_rows, grad_pairs[h, p]),
        [penalty(listed, p, w) for w in places],
        finals[h, p : p + 1, :],
        finals[h, 4 + p : 5 + p, :],
    )
    dk = matmul(score_grad, query_pairs[h, p])
    dv = matmul(half, grad_pairs[h, p])
    return dk, dv, diagonal(matmul(key_turned, score_grad))


def edge_kernel(
    listed, finals, query_pairs, grad_pairs, dq_in, from_up, from_down, from_left, from_right,
    up_sum, down_sum, left_back, right_back, dq_out,
):
    ends = ((from_up, UP), (from_down, DOWN))
    sides = ((from_left, LEFT), (from_right, RIGHT))

    def step(h, carry):
        def rows(source, n):
            return source[n, :, :, cols(h)].reshape(256, 128)

        end_sums, side_sums = [0.0, 0.0], [0.0, 0.0]
        for p in range(4):
            s, c = p // 2, p % 2
            pair = ends[s], sides[c]
            key_rows = jnp.concatenate([rows(source, 0) for source, _ in pair], axis=0)
            value_rows = jnp.concatenate([rows(source, 1) for source, _ in pair], axis=0)
            dk, dv, dq = patch_gradients(
                h, p, key_rows, value_rows, key_rows.T, listed, pair[0][1] + pair[1][1],
                finals, query_pairs, grad_pairs,
            )
            dq_out[h, p] = dq_in[h, p] + dq
            both = jnp.concatenate([dk, dv], axis=1)
            end_sums[s] = end_sums[s] + both[:256]
            side_sums[c] = side_sums[c] + both[256:]
        for s, back in enumerate((up_sum, down_sum)):
            for at in range(2):
                for n in range(2):
                    back[n, at, :, cols(h)] = end_sums[s][128 * at : 128 * (at + 1), 128 * n : 128 * (n + 1)]
        for c, back in enumerate((left_back, right_back)):
            for at in range(2):
                for n in range(2):
                    part = side_sums[c][128 * at : 128 * (at + 1), 128 * n : 128 * (n + 1)]
                    back[n, at, :, cols(h)] = part.astype(jnp.bfloat16)
        return carry

    lax.fori_loop(0, PAIRS, step, 0)


def add_kernel(up_sum, down_sum, add_left, add_right, up_back, down_back):
    for n in range(2):
        for s, (total, back) in enumerate(((up_sum, up_back), (down_sum, down_back))):
            for at, added in enumerate((add_left, add_right)):
                back[n, at] = (total[n, at] + added[n, s].astype(jnp.float32)).astype(jnp.bfloat16)


def last_kernel(own_key, own_value, left, right, up, down, key_grad, value_grad):
    for n, (own, out) in enumerate(((own_key, key_grad), (own_value, value_grad))):
        for p in range(4):
            s, c = p // 2, p % 2
            beside = (left, right)[c][n, s].astype(jnp.float32)
            end = (up, down)[s][n, c].astype(jnp.float32)
            total = own[128 * p : 128 * (p + 1), :] + beside + end
            out[s, c] = total.astype(jnp.bfloat16)


def own_kernel(
    listed, finals, query_pairs, grad_pairs, key, value, dq_in, own_key, own_value, query_grad
):
    def step(h, carry):
        key_rows, value_rows = key[:, cols(h)], value[:, cols(h)]
        key_turned = key_rows.T
        joined_query = jnp.concatenate([query_pairs[h, p] for p in range(4)], axis=0)
        joined_grad = jnp.concatenate([grad_pairs[h, p] for p in range(4)], axis=0)
        terms = [
            gradients(
                product(key_rows, query_pairs[h, p]),
                product(value_rows, grad_pairs[h, p]),
                [penalty(listed, p, w) for w in OWN],
                finals[h, p : p + 1, :],
                finals[h, 4 + p : 5 + p, :],
            )
            for p in range(4)
        ]
        dq = [diagonal(matmul(key_turned, score_grad)) for _, score_grad in terms]
        dk = matmul(jnp.concatenate([score_grad for _, score_grad in terms], axis=1), joined_query)
        dv = matmul(jnp.concatenate([half for half, _ in terms], axis=1), joined_grad)
        for p in range(4):
            query_grad[p, :, cols(h)] = (SCALING * (dq_in[h, p] + dq[p]).T).astype(jnp.bfloat16)
        own_key[:, cols(h)] = dk
        own_value[:, cols(h)] = dv
        return carry

    lax.fori_loop(0, PAIRS, step, 0)


BF16, F32 = jnp.bfloat16, jnp.float32
TILE = (PATCH, D)
IN_VMEM = pl.BlockSpec(memory_space=pltpu.VMEM)
IN_SMEM = pl.BlockSpec(memory_space=pltpu.SMEM)


def call(kernel, outs, flops, *args):
    def space(kind):
        return IN_SMEM if kind == jnp.int32 else IN_VMEM

    return pl.pallas_call(
        kernel,
        out_shape=[jax.ShapeDtypeStruct(shape, kind) for shape, kind in outs],
        in_specs=[space(x.dtype) for x in args],
        out_specs=[space(kind) for _, kind in outs],
        compiler_params=pltpu.CompilerParams(vmem_limit_bytes=40 * 1024 * 1024),
        cost_estimate=pl.CostEstimate(flops=flops, bytes_accessed=10**6, transcendentals=0),
    )(*args)


PAIR_SHAPE = ((PAIRS, 4, 256, 128), BF16)
TURNED = ((PAIRS, 4, 128, PATCH), F32)
STATS = ((PAIRS, 8, 256), F32)
TWO = ((2, 2) + TILE, BF16)


def local(query_tiles, key_tiles, value_tiles, out_grad, mix_gain, partners, counts):
    span_total, chord_total = 2 * lax.axis_size("span"), 2 * lax.axis_size("chord")
    every = slice(None)

    def packed(tiles, *index):
        return jnp.stack([x[index] for x in tiles])

    from_up = shifted(packed((key_tiles, value_tiles), 1), 1, 0)
    from_down = shifted(packed((key_tiles, value_tiles), 0), -1, 0)
    from_left = shifted(packed((key_tiles, value_tiles, out_grad), every, 1), 0, 1)
    from_right = shifted(packed((key_tiles, value_tiles, out_grad), every, 0), 0, -1)

    def corners(c):
        return jnp.stack([from_up[:, c], from_down[:, c]], axis=1)

    for_left, for_right = corners(0), corners(1)
    corner_left = shifted(for_right, 0, 1)
    corner_right = shifted(for_left, 0, -1)

    key_rows, value_rows = key_tiles.reshape(4 * PATCH, D), value_tiles.reshape(4 * PATCH, D)
    listed, query_pairs, stats, attended = call(
        functools.partial(own_totals_kernel, chord_total),
        [((72,), jnp.int32), PAIR_SHAPE, STATS, TURNED], 6 * 10**9,
        partners, counts, query_tiles.reshape((4,) + TILE), key_rows, value_rows,
    )
    upper, lower, *_ = lax.optimization_barrier((out_grad[0], out_grad[1], for_left, for_right))
    grad_up, grad_down = shifted(lower, 1, 0), shifted(upper, -1, 0)
    stats, attended = call(
        edge_totals_kernel, [STATS, TURNED], 6 * 10**9,
        listed, query_pairs, stats, attended, from_up, from_down, from_left, from_right,
    )
    grad_pairs, finals, left_back, right_back, dq = call(
        functools.partial(corner_kernel, span_total, chord_total),
        [PAIR_SHAPE, STATS, TWO, TWO, TURNED], 3 * 10**9,
        listed, partners, mix_gain, out_grad, grad_up, grad_down, from_left, from_right,
        stats, attended, query_pairs, corner_left, corner_right,
    )
    pairs = query_pairs, grad_pairs
    add_right = shifted(left_back, 0, -1)
    add_left = shifted(right_back, 0, 1)
    wide = ((2, 2) + TILE, F32)
    up_sum, down_sum, left_back, right_back, dq = call(
        edge_kernel, [wide, wide, TWO, TWO, TURNED], 8 * 10**9,
        listed, finals, *pairs, dq, from_up, from_down, from_left, from_right,
    )
    up_back, down_back = call(
        add_kernel, [TWO, TWO], 10**7, up_sum, down_sum, add_left, add_right
    )
    end_down = shifted(up_back, -1, 0)
    end_up = shifted(down_back, 1, 0)
    left_back, right_back, *_ = lax.optimization_barrier((left_back, right_back, up_back, down_back))
    side_right = shifted(left_back, 0, -1)
    side_left = shifted(right_back, 0, 1)
    own_key, own_value, query_grad = call(
        own_kernel, [((4 * PATCH, D), F32), ((4 * PATCH, D), F32), ((4,) + TILE, BF16)], 10**10,
        listed, finals, *pairs, key_rows, value_rows, dq,
    )

    key_grad, value_grad = call(
        last_kernel, [TWO, TWO], 10**7,
        own_key, own_value, side_left, side_right, end_up, end_down,
    )
    return (query_grad.reshape((2, 2) + TILE), key_grad, value_grad)


def solution(mesh):
    tiles = P("span", "chord", None, None)
    in_specs = (tiles, tiles, tiles, tiles, P(), P("span", "chord", None), P("span", "chord"))
    return jax.shard_map(
        local, mesh=mesh, in_specs=in_specs, out_specs=(tiles, tiles, tiles), check_vma=False
    )
```

```python
import functools

import jax
import jax.numpy as jnp
from jax import lax
from jax.experimental import pallas as pl
from jax.experimental.pallas import tpu as pltpu
from jax.sharding import PartitionSpec as P

PATCH = 128
D = 512
PAIRS = 4
SCALING = 0.125
LOW_FILL = -1e30
NT = (((1,), (1,)), ((), ()))

OWN = (5, 6, 9, 10)
UP, DOWN, LEFT, RIGHT = (1, 2), (13, 14), (4, 8), (7, 11)
CORNERS = (0, 3, 12, 15)


def shifted(x, span_step, chord_step):
    span, chord = lax.axis_size("span"), lax.axis_size("chord")
    pairs = [
        (s * chord + c, ((s + span_step) % span) * chord + (c + chord_step) % chord)
        for s in range(span)
        for c in range(chord)
    ]
    return lax.ppermute(x, ("span", "chord"), pairs)


def stacked_pair(rows):
    lane = lax.broadcasted_iota(jnp.int32, rows.shape, 1)
    zero = jnp.zeros_like(rows)
    return jnp.concatenate(
        [jnp.where(lane < 64, rows, zero), jnp.where(lane >= 64, rows, zero)], axis=0
    )


def cols(h):
    return pl.ds(pl.multiple_of(h * 128, 128), 128)


def product(rows, pair):
    return lax.dot_general(rows, pair, NT, preferred_element_type=jnp.float32)


def matmul(a, b):
    return jnp.dot(a, b, preferred_element_type=jnp.float32)


def diagonal(x):
    return jnp.concatenate([x[:64, :128], x[64:, 128:]], axis=0)


def per_head(row):
    return jnp.concatenate(
        [jnp.broadcast_to(row[:, :128], (64, 128)), jnp.broadcast_to(row[:, 128:], (64, 128))], axis=0
    )


def penalty(listed, p, w):
    return jnp.where(listed[p * 16 + w] > 0, 0.0, -LOW_FILL)


def exponents(s, row, penalties):
    return jnp.concatenate(
        [jnp.exp(s[128 * i : 128 * (i + 1)] - (row + x)) for i, x in enumerate(penalties)], axis=0
    )


def highest(s, penalties):
    tops = [
        jnp.max(s[128 * i : 128 * (i + 1)], axis=0, keepdims=True) - x for i, x in enumerate(penalties)
    ]
    return functools.reduce(jnp.maximum, tops)


def merged(groups, stats, attended):
    tops = [highest(s, penalties) for s, penalties, _ in groups]
    if stats is not None:
        tops.append(stats[0])
    top = functools.reduce(jnp.maximum, tops)
    total, turned = 0.0, 0.0
    for s, penalties, value_turned in groups:
        e = exponents(s, top, penalties)
        total = total + jnp.sum(e, axis=0, keepdims=True)
        turned = turned + matmul(value_turned, e.astype(jnp.bfloat16))
    turned = diagonal(turned)
    if stats is not None:
        fade = jnp.exp(stats[0] - top)
        total = total + stats[1] * fade
        turned = turned + attended * per_head(fade)
    return top, total, turned


def own_totals_kernel(
    chord_total, partners, counts, query, key, value, listed, query_pairs, stats_out, attended_out
):
    for i in range(72):
        listed[i] = 0
    for p in range(4):
        s, c = p // 2, p % 2
        own = partners[s, c, 0]
        for j in range(8):
            other = partners[s, c, j]
            row = 1 + s + lax.div(other, chord_total) - lax.div(own, chord_total)
            column = 1 + c + lax.rem(other, chord_total) - lax.rem(own, chord_total)
            listed[jnp.where(j < counts[s, c], p * 16 + row * 4 + column, 64)] = 1

    def step(h, carry):
        value_turned = value[:, cols(h)].T

        def groups_of(p):
            pair = stacked_pair(query[p, :, cols(h)] * jnp.bfloat16(SCALING))
            query_pairs[h, p] = pair
            groups = []
            for n in range(2):
                rows = slice(256 * n, 256 * (n + 1))
                groups.append(
                    (
                        product(key[rows, cols(h)], pair),
                        [penalty(listed, p, w) for w in OWN[2 * n : 2 * n + 2]],
                        value_turned[:, rows],
                    )
                )
            return groups

        ahead = groups_of(0)
        for p in range(4):
            groups = ahead
            ahead = groups_of(p + 1) if p < 3 else None
            top, total, turned = merged(groups, None, None)
            stats_out[h, p : p + 1, :] = top
            stats_out[h, 4 + p : 5 + p, :] = total
            attended_out[h, p] = turned
        return carry

    lax.fori_loop(0, PAIRS, step, 0)


def edge_totals_kernel(
    listed, query_pairs, stats_in, attended_in, from_up, from_down, from_left, from_right,
    stats_out, attended_out,
):
    ends = ((from_up, UP), (from_down, DOWN))
    sides = ((from_left, LEFT), (from_right, RIGHT))

    def step(h, carry):
        def turned(source):
            return source[1, :, :, cols(h)].reshape(256, 128).T

        values = {id(source): turned(source) for source, _ in ends + sides}

        def groups_of(p):
            return [
                (
                    product(source[0, :, :, cols(h)].reshape(256, 128), query_pairs[h, p]),
                    [penalty(listed, p, w) for w in places],
                    values[id(source)],
                )
                for source, places in (ends[p // 2], sides[p % 2])
            ]

        ahead = groups_of(0)
        for p in range(4):
            groups = ahead
            ahead = groups_of(p + 1) if p < 3 else None
            stats = stats_in[h, p : p + 1, :], stats_in[h, 4 + p : 5 + p, :]
            top, total, attended = merged(groups, stats, attended_in[h, p])
            stats_out[h, p : p + 1, :] = top
            stats_out[h, 4 + p : 5 + p, :] = total
            attended_out[h, p] = attended
        return carry

    lax.fori_loop(0, PAIRS, step, 0)


def gradients(s, g, penalties, log_total, delta):
    prob = exponents(s, log_total, penalties)
    return prob.astype(jnp.bfloat16), (prob * (g - delta)).astype(jnp.bfloat16)


def corner_kernel(
    span_total, chord_total, listed, partners, gain, grad, grad_up, grad_down, from_left, from_right,
    stats_in, attended_in, query_pairs, corner_left, corner_right,
    grad_pairs, finals, left_back, right_back, dq_out,
):
    first = partners[0, 0, 0]
    row, column = lax.div(first, chord_total), lax.rem(first, chord_total)
    inside = [
        jnp.where(x, 1.0, 0.0)
        for x in (row > 0, row < span_total - 2, column > 0, column < chord_total - 2)
    ]
    patches = range(4)

    def source(p):
        return (corner_left, corner_right)[p % 2]

    def step(h, carry):
        pairs, grad_turned = [], []
        for p in patches:
            s, c = p // 2, p % 2
            near = (
                grad[0, c, :, cols(h)] if s == 1 else grad_up[c, :, cols(h)],
                grad[1, c, :, cols(h)] if s == 0 else grad_down[c, :, cols(h)],
                grad[s, 0, :, cols(h)] if c == 1 else from_left[2, s, :, cols(h)],
                grad[s, 1, :, cols(h)] if c == 0 else from_right[2, s, :, cols(h)],
            )
            own = (s == 1, s == 0, c == 1, c == 0)
            mixed = grad[s, c, :, cols(h)].astype(jnp.float32)
            for n in range(4):
                factor = gain[n : n + 1, cols(h)]
                if not own[n]:
                    factor = factor * inside[n]
                mixed = mixed + factor * near[n].astype(jnp.float32)
            mixed = mixed.astype(jnp.bfloat16)
            pair = stacked_pair(mixed)
            grad_pairs[h, p] = pair
            pairs.append(pair)
            grad_turned.append(mixed.T)
        key_rows = [source(p)[0, p // 2, :, cols(h)] for p in patches]
        value_rows = [source(p)[1, p // 2, :, cols(h)] for p in patches]
        scores = [product(key_rows[p], query_pairs[h, p]) for p in patches]
        g = [product(value_rows[p], pairs[p]) for p in patches]
        value_turned = [x.T for x in value_rows]
        key_turned = [x.T for x in key_rows]
        half, score_grad = [], []
        for p in patches:
            missing = penalty(listed, p, CORNERS[p])
            old_top, old_total = stats_in[h, p : p + 1, :], stats_in[h, 4 + p : 5 + p, :]
            top = jnp.maximum(old_top, jnp.max(scores[p], axis=0, keepdims=True) - missing)
            fade = jnp.exp(old_top - top)
            e = jnp.exp(scores[p] - (top + missing))
            total = old_total * fade + jnp.sum(e, axis=0, keepdims=True)
            attended = diagonal(matmul(value_turned[p], e.astype(jnp.bfloat16)))
            attended = attended + attended_in[h, p] * per_head(fade)
            dots = grad_turned[p].astype(jnp.float32) * attended
            dot = jnp.concatenate(
                [jnp.sum(dots[:64], axis=0, keepdims=True), jnp.sum(dots[64:], axis=0, keepdims=True)], axis=1
            )
            scale = 1.0 / total
            delta = dot * scale
            finals[h, p : p + 1, :] = top + jnp.log(total)
            finals[h, 4 + p : 5 + p, :] = delta
            prob = e * scale
            half.append(prob.astype(jnp.bfloat16))
            score_grad.append((prob * (g[p] - delta)).astype(jnp.bfloat16))
        for p in patches:
            back = (left_back, right_back)[p % 2]
            back[0, p // 2, :, cols(h)] = matmul(score_grad[p], query_pairs[h, p]).astype(jnp.bfloat16)
            back[1, p // 2, :, cols(h)] = matmul(half[p], pairs[p]).astype(jnp.bfloat16)
            dq_out[h, p] = diagonal(matmul(key_turned[p], score_grad[p]))
        return carry

    lax.fori_loop(0, PAIRS, step, 0)


def patch_gradients(h, p, key_rows, value_rows, key_turned, listed, places, finals, query_pairs, grad_pairs):
    half, score_grad = gradients(
        product(key_rows, query_pairs[h, p]),
        product(value_rows, grad_pairs[h, p]),
        [penalty(listed, p, w) for w in places],
        finals[h, p : p + 1, :],
        finals[h, 4 + p : 5 + p, :],
    )
    dk = matmul(score_grad, query_pairs[h, p])
    dv = matmul(half, grad_pairs[h, p])
    return dk, dv, diagonal(matmul(key_turned, score_grad))


def edge_kernel(
    listed, finals, query_pairs, grad_pairs, dq_in, from_up, from_down, from_left, from_right,
    up_sum, down_sum, left_back, right_back, dq_out,
):
    ends = ((from_up, UP), (from_down, DOWN))
    sides = ((from_left, LEFT), (from_right, RIGHT))

    def step(h, carry):
        def rows(source, n):
            return source[n, :, :, cols(h)].reshape(256, 128)

        end_sums, side_sums = [0.0, 0.0], [0.0, 0.0]
        for p in range(4):
            s, c = p // 2, p % 2
            pair = ends[s], sides[c]
            key_rows = jnp.concatenate([rows(source, 0) for source, _ in pair], axis=0)
            value_rows = jnp.concatenate([rows(source, 1) for source, _ in pair], axis=0)
            dk, dv, dq = patch_gradients(
                h, p, key_rows, value_rows, key_rows.T, listed, pair[0][1] + pair[1][1],
                finals, query_pairs, grad_pairs,
            )
            dq_out[h, p] = dq_in[h, p] + dq
            both = jnp.concatenate([dk, dv], axis=1)
            end_sums[s] = end_sums[s] + both[:256]
            side_sums[c] = side_sums[c] + both[256:]
        for s, back in enumerate((up_sum, down_sum)):
            for at in range(2):
                for n in range(2):
                    back[n, at, :, cols(h)] = end_sums[s][128 * at : 128 * (at + 1), 128 * n : 128 * (n + 1)]
        for c, back in enumerate((left_back, right_back)):
            for at in range(2):
                for n in range(2):
                    part = side_sums[c][128 * at : 128 * (at + 1), 128 * n : 128 * (n + 1)]
                    back[n, at, :, cols(h)] = part.astype(jnp.bfloat16)
        return carry

    lax.fori_loop(0, PAIRS, step, 0)


def add_kernel(up_sum, down_sum, add_left, add_right, up_back, down_back):
    for n in range(2):
        for s, (total, back) in enumerate(((up_sum, up_back), (down_sum, down_back))):
            for at, added in enumerate((add_left, add_right)):
                back[n, at] = (total[n, at] + added[n, s].astype(jnp.float32)).astype(jnp.bfloat16)


def last_kernel(own_key, own_value, left, right, up, down, key_grad, value_grad):
    for n, (own, out) in enumerate(((own_key, key_grad), (own_value, value_grad))):
        for p in range(4):
            s, c = p // 2, p % 2
            beside = (left, right)[c][n, s].astype(jnp.float32)
            end = (up, down)[s][n, c].astype(jnp.float32)
            total = own[128 * p : 128 * (p + 1), :] + beside + end
            out[s, c] = total.astype(jnp.bfloat16)


def own_kernel(
    listed, finals, query_pairs, grad_pairs, key, value, dq_in, own_key, own_value, query_grad
):
    def step(h, carry):
        key_rows, value_rows = key[:, cols(h)], value[:, cols(h)]
        key_turned = key_rows.T
        joined_query = jnp.concatenate([query_pairs[h, p] for p in range(4)], axis=0)
        joined_grad = jnp.concatenate([grad_pairs[h, p] for p in range(4)], axis=0)
        terms = [
            gradients(
                product(key_rows, query_pairs[h, p]),
                product(value_rows, grad_pairs[h, p]),
                [penalty(listed, p, w) for w in OWN],
                finals[h, p : p + 1, :],
                finals[h, 4 + p : 5 + p, :],
            )
            for p in range(4)
        ]
        dq = [diagonal(matmul(key_turned, score_grad)) for _, score_grad in terms]
        dk = matmul(jnp.concatenate([score_grad for _, score_grad in terms], axis=1), joined_query)
        dv = matmul(jnp.concatenate([half for half, _ in terms], axis=1), joined_grad)
        for p in range(4):
            query_grad[p, :, cols(h)] = (SCALING * (dq_in[h, p] + dq[p]).T).astype(jnp.bfloat16)
        own_key[:, cols(h)] = dk
        own_value[:, cols(h)] = dv
        return carry

    lax.fori_loop(0, PAIRS, step, 0)


BF16, F32 = jnp.bfloat16, jnp.float32
TILE = (PATCH, D)
IN_VMEM = pl.BlockSpec(memory_space=pltpu.VMEM)
IN_SMEM = pl.BlockSpec(memory_space=pltpu.SMEM)


def call(kernel, outs, flops, *args):
    def space(kind):
        return IN_SMEM if kind == jnp.int32 else IN_VMEM

    return pl.pallas_call(
        kernel,
        out_shape=[jax.ShapeDtypeStruct(shape, kind) for shape, kind in outs],
        in_specs=[space(x.dtype) for x in args],
        out_specs=[space(kind) for _, kind in outs],
        compiler_params=pltpu.CompilerParams(vmem_limit_bytes=40 * 1024 * 1024),
        cost_estimate=pl.CostEstimate(flops=flops, bytes_accessed=10**6, transcendentals=0),
    )(*args)


PAIR_SHAPE = ((PAIRS, 4, 256, 128), BF16)
TURNED = ((PAIRS, 4, 128, PATCH), F32)
STATS = ((PAIRS, 8, 256), F32)
TWO = ((2, 2) + TILE, BF16)


def local(query_tiles, key_tiles, value_tiles, out_grad, mix_gain, partners, counts):
    span_total, chord_total = 2 * lax.axis_size("span"), 2 * lax.axis_size("chord")
    every = slice(None)

    def packed(tiles, *index):
        return jnp.stack([x[index] for x in tiles])

    from_up = shifted(packed((key_tiles, value_tiles), 1), 1, 0)
    from_down = shifted(packed((key_tiles, value_tiles), 0), -1, 0)
    from_left = shifted(packed((key_tiles, value_tiles, out_grad), every, 1), 0, 1)
    from_right = shifted(packed((key_tiles, value_tiles, out_grad), every, 0), 0, -1)

    def corners(c):
        return jnp.stack([from_up[:, c], from_down[:, c]], axis=1)

    corner_left = shifted(corners(1), 0, 1)
    corner_right = shifted(corners(0), 0, -1)

    key_rows, value_rows = key_tiles.reshape(4 * PATCH, D), value_tiles.reshape(4 * PATCH, D)
    listed, query_pairs, stats, attended = call(
        functools.partial(own_totals_kernel, chord_total),
        [((72,), jnp.int32), PAIR_SHAPE, STATS, TURNED], 6 * 10**9,
        partners, counts, query_tiles.reshape((4,) + TILE), key_rows, value_rows,
    )
    upper, lower, stats = lax.optimization_barrier((out_grad[0], out_grad[1], stats))
    grad_up, grad_down = shifted(lower, 1, 0), shifted(upper, -1, 0)
    stats, attended = call(
        edge_totals_kernel, [STATS, TURNED], 6 * 10**9,
        listed, query_pairs, stats, attended, from_up, from_down, from_left, from_right,
    )
    grad_pairs, finals, left_back, right_back, dq = call(
        functools.partial(corner_kernel, span_total, chord_total),
        [PAIR_SHAPE, STATS, TWO, TWO, TURNED], 3 * 10**9,
        listed, partners, mix_gain, out_grad, grad_up, grad_down, from_left, from_right,
        stats, attended, query_pairs, corner_left, corner_right,
    )
    pairs = query_pairs, grad_pairs
    add_right = shifted(left_back, 0, -1)
    add_left = shifted(right_back, 0, 1)
    wide = ((2, 2) + TILE, F32)
    up_sum, down_sum, left_back, right_back, dq = call(
        edge_kernel, [wide, wide, TWO, TWO, TURNED], 8 * 10**9,
        listed, finals, *pairs, dq, from_up, from_down, from_left, from_right,
    )
    up_back, down_back = call(
        add_kernel, [TWO, TWO], 10**7, up_sum, down_sum, add_left, add_right
    )
    end_down = shifted(up_back, -1, 0)
    end_up = shifted(down_back, 1, 0)
    left_back, right_back, *_ = lax.optimization_barrier((left_back, right_back, up_back, down_back))
    side_right = shifted(left_back, 0, -1)
    side_left = shifted(right_back, 0, 1)
    own_key, own_value, query_grad = call(
        own_kernel, [((4 * PATCH, D), F32), ((4 * PATCH, D), F32), ((4,) + TILE, BF16)], 10**10,
        listed, finals, *pairs, key_rows, value_rows, dq,
    )

    key_grad, value_grad = call(
        last_kernel, [TWO, TWO], 10**7,
        own_key, own_value, side_left, side_right, end_up, end_down,
    )
    return (query_grad.reshape((2, 2) + TILE), key_grad, value_grad)


def solution(mesh):
    tiles = P("span", "chord", None, None)
    in_specs = (tiles, tiles, tiles, tiles, P(), P("span", "chord", None), P("span", "chord"))
    return jax.shard_map(
        local, mesh=mesh, in_specs=in_specs, out_specs=(tiles, tiles, tiles), check_vma=False
    )
```

```python
import functools

import jax
import jax.numpy as jnp
from jax import lax
from jax.experimental import pallas as pl
from jax.experimental.pallas import tpu as pltpu
from jax.sharding import PartitionSpec as P

PATCH = 128
D = 512
PAIRS = 4
SCALING = 0.125
LOW_FILL = -1e30
NT = (((1,), (1,)), ((), ()))

OWN = (5, 6, 9, 10)
UP, DOWN, LEFT, RIGHT = (1, 2), (13, 14), (4, 8), (7, 11)
CORNERS = (0, 3, 12, 15)


def shifted(x, span_step, chord_step):
    span, chord = lax.axis_size("span"), lax.axis_size("chord")
    pairs = [
        (s * chord + c, ((s + span_step) % span) * chord + (c + chord_step) % chord)
        for s in range(span)
        for c in range(chord)
    ]
    return lax.ppermute(x, ("span", "chord"), pairs)


def stacked_pair(rows):
    lane = lax.broadcasted_iota(jnp.int32, rows.shape, 1)
    zero = jnp.zeros_like(rows)
    return jnp.concatenate(
        [jnp.where(lane < 64, rows, zero), jnp.where(lane >= 64, rows, zero)], axis=0
    )


def cols(h):
    return pl.ds(pl.multiple_of(h * 128, 128), 128)


def product(rows, pair):
    return lax.dot_general(rows, pair, NT, preferred_element_type=jnp.float32)


def matmul(a, b):
    return jnp.dot(a, b, preferred_element_type=jnp.float32)


def diagonal(x):
    return jnp.concatenate([x[:64, :128], x[64:, 128:]], axis=0)


def per_head(row):
    return jnp.concatenate(
        [jnp.broadcast_to(row[:, :128], (64, 128)), jnp.broadcast_to(row[:, 128:], (64, 128))], axis=0
    )


def penalty(listed, p, w):
    return jnp.where(listed[p * 16 + w] > 0, 0.0, -LOW_FILL)


def exponents(s, row, penalties):
    return jnp.concatenate(
        [jnp.exp(s[128 * i : 128 * (i + 1)] - (row + x)) for i, x in enumerate(penalties)], axis=0
    )


def highest(s, penalties):
    tops = [
        jnp.max(s[128 * i : 128 * (i + 1)], axis=0, keepdims=True) - x for i, x in enumerate(penalties)
    ]
    return functools.reduce(jnp.maximum, tops)


def merged(groups, stats, attended):
    tops = [highest(s, penalties) for s, penalties, _ in groups]
    if stats is not None:
        tops.append(stats[0])
    top = functools.reduce(jnp.maximum, tops)
    total, turned = 0.0, 0.0
    for s, penalties, value_turned in groups:
        e = exponents(s, top, penalties)
        total = total + jnp.sum(e, axis=0, keepdims=True)
        turned = turned + matmul(value_turned, e.astype(jnp.bfloat16))
    turned = diagonal(turned)
    if stats is not None:
        fade = jnp.exp(stats[0] - top)
        total = total + stats[1] * fade
        turned = turned + attended * per_head(fade)
    return top, total, turned


def own_totals_kernel(
    chord_total, partners, counts, query, key, value, listed, query_pairs, stats_out, attended_out
):
    for i in range(72):
        listed[i] = 0
    for p in range(4):
        s, c = p // 2, p % 2
        own = partners[s, c, 0]
        for j in range(8):
            other = partners[s, c, j]
            row = 1 + s + lax.div(other, chord_total) - lax.div(own, chord_total)
            column = 1 + c + lax.rem(other, chord_total) - lax.rem(own, chord_total)
            listed[jnp.where(j < counts[s, c], p * 16 + row * 4 + column, 64)] = 1

    def step(h, carry):
        value_turned = value[:, cols(h)].T

        def groups_of(p):
            pair = stacked_pair(query[p, :, cols(h)] * jnp.bfloat16(SCALING))
            query_pairs[h, p] = pair
            groups = []
            for n in range(2):
                rows = slice(256 * n, 256 * (n + 1))
                groups.append(
                    (
                        product(key[rows, cols(h)], pair),
                        [penalty(listed, p, w) for w in OWN[2 * n : 2 * n + 2]],
                        value_turned[:, rows],
                    )
                )
            return groups

        ahead = groups_of(0)
        for p in range(4):
            groups = ahead
            ahead = groups_of(p + 1) if p < 3 else None
            top, total, turned = merged(groups, None, None)
            stats_out[h, p : p + 1, :] = top
            stats_out[h, 4 + p : 5 + p, :] = total
            attended_out[h, p] = turned
        return carry

    lax.fori_loop(0, PAIRS, step, 0)


def edge_totals_kernel(
    listed, query_pairs, stats_in, attended_in, from_up, from_down, from_left, from_right,
    stats_out, attended_out,
):
    ends = ((from_up, UP), (from_down, DOWN))
    sides = ((from_left, LEFT), (from_right, RIGHT))

    def step(h, carry):
        def turned(source):
            return source[1, :, :, cols(h)].reshape(256, 128).T

        values = {id(source): turned(source) for source, _ in ends + sides}

        def groups_of(p):
            return [
                (
                    product(source[0, :, :, cols(h)].reshape(256, 128), query_pairs[h, p]),
                    [penalty(listed, p, w) for w in places],
                    values[id(source)],
                )
                for source, places in (ends[p // 2], sides[p % 2])
            ]

        ahead = groups_of(0)
        for p in range(4):
            groups = ahead
            ahead = groups_of(p + 1) if p < 3 else None
            stats = stats_in[h, p : p + 1, :], stats_in[h, 4 + p : 5 + p, :]
            top, total, attended = merged(groups, stats, attended_in[h, p])
            stats_out[h, p : p + 1, :] = top
            stats_out[h, 4 + p : 5 + p, :] = total
            attended_out[h, p] = attended
        return carry

    lax.fori_loop(0, PAIRS, step, 0)


def gradients(s, g, penalties, log_total, delta):
    prob = exponents(s, log_total, penalties)
    return prob.astype(jnp.bfloat16), (prob * (g - delta)).astype(jnp.bfloat16)


def mixed_kernel(
    span_total, chord_total, partners, gain, grad, grad_up, grad_down, from_left, from_right, after,
    grad_pairs, grad_turned,
):
    first = partners[0, 0, 0]
    row, column = lax.div(first, chord_total), lax.rem(first, chord_total)
    inside = [
        jnp.where(x, 1.0, 0.0)
        for x in (row > 0, row < span_total - 2, column > 0, column < chord_total - 2)
    ]

    def step(h, carry):
        for p in range(4):
            s, c = p // 2, p % 2
            near = (
                grad[0, c, :, cols(h)] if s == 1 else grad_up[c, :, cols(h)],
                grad[1, c, :, cols(h)] if s == 0 else grad_down[c, :, cols(h)],
                grad[s, 0, :, cols(h)] if c == 1 else from_left[2, s, :, cols(h)],
                grad[s, 1, :, cols(h)] if c == 0 else from_right[2, s, :, cols(h)],
            )
            own = (s == 1, s == 0, c == 1, c == 0)
            mixed = grad[s, c, :, cols(h)].astype(jnp.float32)
            for n in range(4):
                factor = gain[n : n + 1, cols(h)]
                if not own[n]:
                    factor = factor * inside[n]
                mixed = mixed + factor * near[n].astype(jnp.float32)
            mixed = mixed.astype(jnp.bfloat16)
            grad_pairs[h, p] = stacked_pair(mixed)
            grad_turned[h, p] = mixed.T
        return carry

    lax.fori_loop(0, PAIRS, step, 0)


def corner_kernel(
    listed, stats_in, attended_in, query_pairs, grad_pairs, grad_turned, corner_left, corner_right,
    finals, left_back, right_back, score_grads,
):
    patches = range(4)

    def source(p):
        return (corner_left, corner_right)[p % 2]

    def step(h, carry):
        key_rows = [source(p)[0, p // 2, :, cols(h)] for p in patches]
        value_rows = [source(p)[1, p // 2, :, cols(h)] for p in patches]
        scores = [product(key_rows[p], query_pairs[h, p]) for p in patches]
        g = [product(value_rows[p], grad_pairs[h, p]) for p in patches]
        value_turned = [x.T for x in value_rows]
        half, score_grad = [], []
        for p in patches:
            missing = penalty(listed, p, CORNERS[p])
            old_top, old_total = stats_in[h, p : p + 1, :], stats_in[h, 4 + p : 5 + p, :]
            top = jnp.maximum(old_top, jnp.max(scores[p], axis=0, keepdims=True) - missing)
            fade = jnp.exp(old_top - top)
            e = jnp.exp(scores[p] - (top + missing))
            total = old_total * fade + jnp.sum(e, axis=0, keepdims=True)
            attended = diagonal(matmul(value_turned[p], e.astype(jnp.bfloat16)))
            attended = attended + attended_in[h, p] * per_head(fade)
            dots = grad_turned[h, p].astype(jnp.float32) * attended
            dot = jnp.concatenate(
                [jnp.sum(dots[:64], axis=0, keepdims=True), jnp.sum(dots[64:], axis=0, keepdims=True)], axis=1
            )
            scale = 1.0 / total
            delta = dot * scale
            finals[h, p : p + 1, :] = top + jnp.log(total)
            finals[h, 4 + p : 5 + p, :] = delta
            prob = e * scale
            half.append(prob.astype(jnp.bfloat16))
            score_grad.append((prob * (g[p] - delta)).astype(jnp.bfloat16))
        for p in patches:
            back = (left_back, right_back)[p % 2]
            back[0, p // 2, :, cols(h)] = matmul(score_grad[p], query_pairs[h, p]).astype(jnp.bfloat16)
            back[1, p // 2, :, cols(h)] = matmul(half[p], grad_pairs[h, p]).astype(jnp.bfloat16)
            score_grads[h, p] = score_grad[p]
        return carry

    lax.fori_loop(0, PAIRS, step, 0)


def patch_gradients(h, p, key_rows, value_rows, key_turned, listed, places, finals, query_pairs, grad_pairs):
    half, score_grad = gradients(
        product(key_rows, query_pairs[h, p]),
        product(value_rows, grad_pairs[h, p]),
        [penalty(listed, p, w) for w in places],
        finals[h, p : p + 1, :],
        finals[h, 4 + p : 5 + p, :],
    )
    dk = matmul(score_grad, query_pairs[h, p])
    dv = matmul(half, grad_pairs[h, p])
    return dk, dv, diagonal(matmul(key_turned, score_grad))


def edge_kernel(
    listed, finals, query_pairs, grad_pairs, score_grads, corner_left, corner_right,
    from_up, from_down, from_left, from_right,
    up_sum, down_sum, left_back, right_back, dq_out,
):
    ends = ((from_up, UP), (from_down, DOWN))
    sides = ((from_left, LEFT), (from_right, RIGHT))

    def step(h, carry):
        def rows(source, n):
            return source[n, :, :, cols(h)].reshape(256, 128)

        end_sums, side_sums = [0.0, 0.0], [0.0, 0.0]
        for p in range(4):
            s, c = p // 2, p % 2
            pair = ends[s], sides[c]
            key_rows = jnp.concatenate([rows(source, 0) for source, _ in pair], axis=0)
            value_rows = jnp.concatenate([rows(source, 1) for source, _ in pair], axis=0)
            dk, dv, dq = patch_gradients(
                h, p, key_rows, value_rows, key_rows.T, listed, pair[0][1] + pair[1][1],
                finals, query_pairs, grad_pairs,
            )
            corner_rows = (corner_left, corner_right)[c][0, s, :, cols(h)]
            dq_out[h, p] = dq + diagonal(matmul(corner_rows.T, score_grads[h, p]))
            both = jnp.concatenate([dk, dv], axis=1)
            end_sums[s] = end_sums[s] + both[:256]
            side_sums[c] = side_sums[c] + both[256:]
        for s, back in enumerate((up_sum, down_sum)):
            for at in range(2):
                for n in range(2):
                    back[n, at, :, cols(h)] = end_sums[s][128 * at : 128 * (at + 1), 128 * n : 128 * (n + 1)]
        for c, back in enumerate((left_back, right_back)):
            for at in range(2):
                for n in range(2):
                    part = side_sums[c][128 * at : 128 * (at + 1), 128 * n : 128 * (n + 1)]
                    back[n, at, :, cols(h)] = part.astype(jnp.bfloat16)
        return carry

    lax.fori_loop(0, PAIRS, step, 0)


def add_kernel(up_sum, down_sum, add_left, add_right, up_back, down_back):
    for n in range(2):
        for s, (total, back) in enumerate(((up_sum, up_back), (down_sum, down_back))):
            for at, added in enumerate((add_left, add_right)):
                back[n, at] = (total[n, at] + added[n, s].astype(jnp.float32)).astype(jnp.bfloat16)


def last_kernel(own_key, own_value, left, right, up, down, key_grad, value_grad):
    for n, (own, out) in enumerate(((own_key, key_grad), (own_value, value_grad))):
        for p in range(4):
            s, c = p // 2, p % 2
            beside = (left, right)[c][n, s].astype(jnp.float32)
            end = (up, down)[s][n, c].astype(jnp.float32)
            total = own[128 * p : 128 * (p + 1), :] + beside + end
            out[s, c] = total.astype(jnp.bfloat16)


def own_kernel(
    listed, finals, query_pairs, grad_pairs, key, value, dq_in, own_key, own_value, query_grad
):
    def step(h, carry):
        key_rows, value_rows = key[:, cols(h)], value[:, cols(h)]
        key_turned = key_rows.T
        joined_query = jnp.concatenate([query_pairs[h, p] for p in range(4)], axis=0)
        joined_grad = jnp.concatenate([grad_pairs[h, p] for p in range(4)], axis=0)
        terms = [
            gradients(
                product(key_rows, query_pairs[h, p]),
                product(value_rows, grad_pairs[h, p]),
                [penalty(listed, p, w) for w in OWN],
                finals[h, p : p + 1, :],
                finals[h, 4 + p : 5 + p, :],
            )
            for p in range(4)
        ]
        dq = [diagonal(matmul(key_turned, score_grad)) for _, score_grad in terms]
        dk = matmul(jnp.concatenate([score_grad for _, score_grad in terms], axis=1), joined_query)
        dv = matmul(jnp.concatenate([half for half, _ in terms], axis=1), joined_grad)
        for p in range(4):
            query_grad[p, :, cols(h)] = (SCALING * (dq_in[h, p] + dq[p]).T).astype(jnp.bfloat16)
        own_key[:, cols(h)] = dk
        own_value[:, cols(h)] = dv
        return carry

    lax.fori_loop(0, PAIRS, step, 0)


BF16, F32 = jnp.bfloat16, jnp.float32
TILE = (PATCH, D)
IN_VMEM = pl.BlockSpec(memory_space=pltpu.VMEM)
IN_SMEM = pl.BlockSpec(memory_space=pltpu.SMEM)


def call(kernel, outs, flops, *args):
    def space(kind):
        return IN_SMEM if kind == jnp.int32 else IN_VMEM

    return pl.pallas_call(
        kernel,
        out_shape=[jax.ShapeDtypeStruct(shape, kind) for shape, kind in outs],
        in_specs=[space(x.dtype) for x in args],
        out_specs=[space(kind) for _, kind in outs],
        compiler_params=pltpu.CompilerParams(vmem_limit_bytes=40 * 1024 * 1024),
        cost_estimate=pl.CostEstimate(flops=flops, bytes_accessed=10**6, transcendentals=0),
    )(*args)


PAIR_SHAPE = ((PAIRS, 4, 256, 128), BF16)
TURNED = ((PAIRS, 4, 128, PATCH), F32)
STATS = ((PAIRS, 8, 256), F32)
TWO = ((2, 2) + TILE, BF16)


def local(query_tiles, key_tiles, value_tiles, out_grad, mix_gain, partners, counts):
    span_total, chord_total = 2 * lax.axis_size("span"), 2 * lax.axis_size("chord")
    every = slice(None)

    def packed(tiles, *index):
        return jnp.stack([x[index] for x in tiles])

    from_up = shifted(packed((key_tiles, value_tiles), 1), 1, 0)
    from_down = shifted(packed((key_tiles, value_tiles), 0), -1, 0)
    for_left = packed((key_tiles, value_tiles, out_grad), every, 0)
    for_right = packed((key_tiles, value_tiles, out_grad), every, 1)
    from_left, from_right = shifted(for_right, 0, 1), shifted(for_left, 0, -1)

    def corners(c):
        return jnp.stack([from_up[:, c], from_down[:, c]], axis=1)

    corner_left = shifted(corners(1), 0, 1)
    corner_right = shifted(corners(0), 0, -1)

    key_rows, value_rows = key_tiles.reshape(4 * PATCH, D), value_tiles.reshape(4 * PATCH, D)
    listed, query_pairs, stats, attended = call(
        functools.partial(own_totals_kernel, chord_total),
        [((72,), jnp.int32), PAIR_SHAPE, STATS, TURNED], 6 * 10**9,
        partners, counts, query_tiles.reshape((4,) + TILE), key_rows, value_rows,
    )
    upper, lower, *_ = lax.optimization_barrier((out_grad[0], out_grad[1], for_left, for_right))
    grad_up, grad_down = shifted(lower, 1, 0), shifted(upper, -1, 0)
    stats, attended = call(
        edge_totals_kernel, [STATS, TURNED], 6 * 10**9,
        listed, query_pairs, stats, attended, from_up, from_down, from_left, from_right,
    )
    grad_pairs, grad_turned = call(
        functools.partial(mixed_kernel, span_total, chord_total),
        [PAIR_SHAPE, ((PAIRS, 4, 128, PATCH), BF16)], 10**9,
        partners, mix_gain, out_grad, grad_up, grad_down, from_left, from_right, stats,
    )
    finals, left_back, right_back, score_grads = call(
        corner_kernel, [STATS, TWO, TWO, ((PAIRS, 4, PATCH, 256), BF16)], 2 * 10**9,
        listed, stats, attended, query_pairs, grad_pairs, grad_turned, corner_left, corner_right,
    )
    pairs = query_pairs, grad_pairs
    add_right = shifted(left_back, 0, -1)
    add_left = shifted(right_back, 0, 1)
    wide = ((2, 2) + TILE, F32)
    up_sum, down_sum, left_back, right_back, dq = call(
        edge_kernel, [wide, wide, TWO, TWO, TURNED], 8 * 10**9,
        listed, finals, *pairs, score_grads, corner_left, corner_right,
        from_up, from_down, from_left, from_right,
    )
    up_back, down_back = call(
        add_kernel, [TWO, TWO], 10**7, up_sum, down_sum, add_left, add_right
    )
    end_down = shifted(up_back, -1, 0)
    end_up = shifted(down_back, 1, 0)
    left_back, right_back, *_ = lax.optimization_barrier((left_back, right_back, up_back, down_back))
    side_right = shifted(left_back, 0, -1)
    side_left = shifted(right_back, 0, 1)
    own_key, own_value, query_grad = call(
        own_kernel, [((4 * PATCH, D), F32), ((4 * PATCH, D), F32), ((4,) + TILE, BF16)], 10**10,
        listed, finals, *pairs, key_rows, value_rows, dq,
    )

    key_grad, value_grad = call(
        last_kernel, [TWO, TWO], 10**7,
        own_key, own_value, side_left, side_right, end_up, end_down,
    )
    return (query_grad.reshape((2, 2) + TILE), key_grad, value_grad)


def solution(mesh):
    tiles = P("span", "chord", None, None)
    in_specs = (tiles, tiles, tiles, tiles, P(), P("span", "chord", None), P("span", "chord"))
    return jax.shard_map(
        local, mesh=mesh, in_specs=in_specs, out_specs=(tiles, tiles, tiles), check_vma=False
    )
```

```python
import functools

import jax
import jax.numpy as jnp
from jax import lax
from jax.experimental import pallas as pl
from jax.experimental.pallas import tpu as pltpu
from jax.sharding import PartitionSpec as P

PATCH = 128
D = 512
PAIRS = 4
SCALING = 0.125
LOW_FILL = -1e30
NT = (((1,), (1,)), ((), ()))

OWN = (5, 6, 9, 10)
UP, DOWN, LEFT, RIGHT = (1, 2), (13, 14), (4, 8), (7, 11)
CORNERS = (0, 3, 12, 15)


def shifted(x, span_step, chord_step):
    span, chord = lax.axis_size("span"), lax.axis_size("chord")
    pairs = [
        (s * chord + c, ((s + span_step) % span) * chord + (c + chord_step) % chord)
        for s in range(span)
        for c in range(chord)
    ]
    return lax.ppermute(x, ("span", "chord"), pairs)


def stacked_pair(rows):
    lane = lax.broadcasted_iota(jnp.int32, rows.shape, 1)
    zero = jnp.zeros_like(rows)
    return jnp.concatenate(
        [jnp.where(lane < 64, rows, zero), jnp.where(lane >= 64, rows, zero)], axis=0
    )


def cols(h):
    return pl.ds(pl.multiple_of(h * 128, 128), 128)


def product(rows, pair):
    return lax.dot_general(rows, pair, NT, preferred_element_type=jnp.float32)


def matmul(a, b):
    return jnp.dot(a, b, preferred_element_type=jnp.float32)


def diagonal(x):
    return jnp.concatenate([x[:64, :128], x[64:, 128:]], axis=0)


def per_head(row):
    return jnp.concatenate(
        [jnp.broadcast_to(row[:, :128], (64, 128)), jnp.broadcast_to(row[:, 128:], (64, 128))], axis=0
    )


def penalty(listed, p, w):
    return jnp.where(listed[p * 16 + w] > 0, 0.0, -LOW_FILL)


def exponents(s, row, penalties):
    return jnp.concatenate(
        [jnp.exp(s[128 * i : 128 * (i + 1)] - (row + x)) for i, x in enumerate(penalties)], axis=0
    )


def highest(s, penalties):
    tops = [
        jnp.max(s[128 * i : 128 * (i + 1)], axis=0, keepdims=True) - x for i, x in enumerate(penalties)
    ]
    return functools.reduce(jnp.maximum, tops)


def merged(groups, stats, attended):
    tops = [highest(s, penalties) for s, penalties, _ in groups]
    if stats is not None:
        tops.append(stats[0])
    top = functools.reduce(jnp.maximum, tops)
    total, turned = 0.0, 0.0
    for s, penalties, value_turned in groups:
        e = exponents(s, top, penalties)
        total = total + jnp.sum(e, axis=0, keepdims=True)
        turned = turned + matmul(value_turned, e.astype(jnp.bfloat16))
    turned = diagonal(turned)
    if stats is not None:
        fade = jnp.exp(stats[0] - top)
        total = total + stats[1] * fade
        turned = turned + attended * per_head(fade)
    return top, total, turned


def own_totals_kernel(
    chord_total, partners, counts, query, key, value, listed, query_pairs, stats_out, attended_out
):
    for i in range(72):
        listed[i] = 0
    for p in range(4):
        s, c = p // 2, p % 2
        own = partners[s, c, 0]
        for j in range(8):
            other = partners[s, c, j]
            row = 1 + s + lax.div(other, chord_total) - lax.div(own, chord_total)
            column = 1 + c + lax.rem(other, chord_total) - lax.rem(own, chord_total)
            listed[jnp.where(j < counts[s, c], p * 16 + row * 4 + column, 64)] = 1

    def step(h, carry):
        value_turned = value[:, cols(h)].T

        def groups_of(p):
            pair = stacked_pair(query[p, :, cols(h)] * jnp.bfloat16(SCALING))
            query_pairs[h, p] = pair
            groups = []
            for n in range(2):
                rows = slice(256 * n, 256 * (n + 1))
                groups.append(
                    (
                        product(key[rows, cols(h)], pair),
                        [penalty(listed, p, w) for w in OWN[2 * n : 2 * n + 2]],
                        value_turned[:, rows],
                    )
                )
            return groups

        ahead = groups_of(0)
        for p in range(4):
            groups = ahead
            ahead = groups_of(p + 1) if p < 3 else None
            top, total, turned = merged(groups, None, None)
            stats_out[h, p : p + 1, :] = top
            stats_out[h, 4 + p : 5 + p, :] = total
            attended_out[h, p] = turned
        return carry

    lax.fori_loop(0, PAIRS, step, 0)


def edge_totals_kernel(
    listed, query_pairs, stats_in, attended_in, from_up, from_down, from_left, from_right,
    stats_out, attended_out,
):
    ends = ((from_up, UP), (from_down, DOWN))
    sides = ((from_left, LEFT), (from_right, RIGHT))

    def step(h, carry):
        def turned(source):
            return source[1, :, :, cols(h)].reshape(256, 128).T

        values = {id(source): turned(source) for source, _ in ends + sides}

        def groups_of(p):
            return [
                (
                    product(source[0, :, :, cols(h)].reshape(256, 128), query_pairs[h, p]),
                    [penalty(listed, p, w) for w in places],
                    values[id(source)],
                )
                for source, places in (ends[p // 2], sides[p % 2])
            ]

        ahead = groups_of(0)
        for p in range(4):
            groups = ahead
            ahead = groups_of(p + 1) if p < 3 else None
            stats = stats_in[h, p : p + 1, :], stats_in[h, 4 + p : 5 + p, :]
            top, total, attended = merged(groups, stats, attended_in[h, p])
            stats_out[h, p : p + 1, :] = top
            stats_out[h, 4 + p : 5 + p, :] = total
            attended_out[h, p] = attended
        return carry

    lax.fori_loop(0, PAIRS, step, 0)


def gradients(s, g, penalties, log_total, delta):
    prob = exponents(s, log_total, penalties)
    return prob.astype(jnp.bfloat16), (prob * (g - delta)).astype(jnp.bfloat16)


def mixed_kernel(
    span_total, chord_total, partners, gain, grad, grad_up, grad_down, from_left, from_right, after,
    grad_pairs, grad_turned,
):
    first = partners[0, 0, 0]
    row, column = lax.div(first, chord_total), lax.rem(first, chord_total)
    inside = [
        jnp.where(x, 1.0, 0.0)
        for x in (row > 0, row < span_total - 2, column > 0, column < chord_total - 2)
    ]

    def step(h, carry):
        for p in range(4):
            s, c = p // 2, p % 2
            near = (
                grad[0, c, :, cols(h)] if s == 1 else grad_up[c, :, cols(h)],
                grad[1, c, :, cols(h)] if s == 0 else grad_down[c, :, cols(h)],
                grad[s, 0, :, cols(h)] if c == 1 else from_left[2, s, :, cols(h)],
                grad[s, 1, :, cols(h)] if c == 0 else from_right[2, s, :, cols(h)],
            )
            own = (s == 1, s == 0, c == 1, c == 0)
            mixed = grad[s, c, :, cols(h)].astype(jnp.float32)
            for n in range(4):
                factor = gain[n : n + 1, cols(h)]
                if not own[n]:
                    factor = factor * inside[n]
                mixed = mixed + factor * near[n].astype(jnp.float32)
            mixed = mixed.astype(jnp.bfloat16)
            grad_pairs[h, p] = stacked_pair(mixed)
            grad_turned[h, p] = mixed.T
        return carry

    lax.fori_loop(0, PAIRS, step, 0)


def corner_kernel(
    listed, stats_in, attended_in, query_pairs, grad_pairs, grad_turned, corner_left, corner_right,
    finals, left_back, right_back, score_grads,
):
    patches = range(4)

    def source(p):
        return (corner_left, corner_right)[p % 2]

    def step(h, carry):
        key_rows = [source(p)[0, p // 2, :, cols(h)] for p in patches]
        value_rows = [source(p)[1, p // 2, :, cols(h)] for p in patches]
        scores = [product(key_rows[p], query_pairs[h, p]) for p in patches]
        g = [product(value_rows[p], grad_pairs[h, p]) for p in patches]
        value_turned = [x.T for x in value_rows]
        half, score_grad = [], []
        for p in patches:
            missing = penalty(listed, p, CORNERS[p])
            old_top, old_total = stats_in[h, p : p + 1, :], stats_in[h, 4 + p : 5 + p, :]
            top = jnp.maximum(old_top, jnp.max(scores[p], axis=0, keepdims=True) - missing)
            fade = jnp.exp(old_top - top)
            e = jnp.exp(scores[p] - (top + missing))
            total = old_total * fade + jnp.sum(e, axis=0, keepdims=True)
            attended = diagonal(matmul(value_turned[p], e.astype(jnp.bfloat16)))
            attended = attended + attended_in[h, p] * per_head(fade)
            dots = grad_turned[h, p].astype(jnp.float32) * attended
            dot = jnp.concatenate(
                [jnp.sum(dots[:64], axis=0, keepdims=True), jnp.sum(dots[64:], axis=0, keepdims=True)], axis=1
            )
            scale = 1.0 / total
            delta = dot * scale
            finals[h, p : p + 1, :] = top + jnp.log(total)
            finals[h, 4 + p : 5 + p, :] = delta
            prob = e * scale
            half.append(prob.astype(jnp.bfloat16))
            score_grad.append((prob * (g[p] - delta)).astype(jnp.bfloat16))
        for p in patches:
            back = (left_back, right_back)[p % 2]
            back[0, p // 2, :, cols(h)] = matmul(score_grad[p], query_pairs[h, p]).astype(jnp.bfloat16)
            back[1, p // 2, :, cols(h)] = matmul(half[p], grad_pairs[h, p]).astype(jnp.bfloat16)
            score_grads[h, p] = score_grad[p]
        return carry

    lax.fori_loop(0, PAIRS, step, 0)


def patch_gradients(h, p, key_rows, value_rows, key_turned, listed, places, finals, query_pairs, grad_pairs):
    half, score_grad = gradients(
        product(key_rows, query_pairs[h, p]),
        product(value_rows, grad_pairs[h, p]),
        [penalty(listed, p, w) for w in places],
        finals[h, p : p + 1, :],
        finals[h, 4 + p : 5 + p, :],
    )
    dk = matmul(score_grad, query_pairs[h, p])
    dv = matmul(half, grad_pairs[h, p])
    return dk, dv, diagonal(matmul(key_turned, score_grad))


def edge_kernel(
    listed, finals, query_pairs, grad_pairs, score_grads, corner_left, corner_right,
    from_up, from_down, from_left, from_right,
    up_sum, down_sum, left_back, right_back, dq_out,
):
    ends = ((from_up, UP), (from_down, DOWN))
    sides = ((from_left, LEFT), (from_right, RIGHT))

    def step(h, carry):
        def rows(source, n):
            return source[n, :, :, cols(h)].reshape(256, 128)

        end_sums, side_sums = [0.0, 0.0], [0.0, 0.0]
        for p in range(4):
            s, c = p // 2, p % 2
            pair = ends[s], sides[c]
            key_rows = jnp.concatenate([rows(source, 0) for source, _ in pair], axis=0)
            value_rows = jnp.concatenate([rows(source, 1) for source, _ in pair], axis=0)
            dk, dv, dq = patch_gradients(
                h, p, key_rows, value_rows, key_rows.T, listed, pair[0][1] + pair[1][1],
                finals, query_pairs, grad_pairs,
            )
            corner_rows = (corner_left, corner_right)[c][0, s, :, cols(h)]
            dq_out[h, p] = dq + diagonal(matmul(corner_rows.T, score_grads[h, p]))
            both = jnp.concatenate([dk, dv], axis=1)
            end_sums[s] = end_sums[s] + both[:256]
            side_sums[c] = side_sums[c] + both[256:]
        for s, back in enumerate((up_sum, down_sum)):
            for at in range(2):
                for n in range(2):
                    back[n, at, :, cols(h)] = end_sums[s][128 * at : 128 * (at + 1), 128 * n : 128 * (n + 1)]
        for c, back in enumerate((left_back, right_back)):
            for at in range(2):
                for n in range(2):
                    part = side_sums[c][128 * at : 128 * (at + 1), 128 * n : 128 * (n + 1)]
                    back[n, at, :, cols(h)] = part.astype(jnp.bfloat16)
        return carry

    lax.fori_loop(0, PAIRS, step, 0)


def add_kernel(up_sum, down_sum, add_left, add_right, up_back, down_back):
    for n in range(2):
        for s, (total, back) in enumerate(((up_sum, up_back), (down_sum, down_back))):
            for at, added in enumerate((add_left, add_right)):
                back[n, at] = (total[n, at] + added[n, s].astype(jnp.float32)).astype(jnp.bfloat16)


def last_kernel(own_key, own_value, left, right, up, down, key_grad, value_grad):
    for n, (own, out) in enumerate(((own_key, key_grad), (own_value, value_grad))):
        for p in range(4):
            s, c = p // 2, p % 2
            beside = (left, right)[c][n, s].astype(jnp.float32)
            end = (up, down)[s][n, c].astype(jnp.float32)
            total = own[128 * p : 128 * (p + 1), :] + beside + end
            out[s, c] = total.astype(jnp.bfloat16)


def own_kernel(
    listed, finals, query_pairs, grad_pairs, key, value, dq_in, own_key, own_value, query_grad
):
    def step(h, carry):
        key_rows, value_rows = key[:, cols(h)], value[:, cols(h)]
        key_turned = key_rows.T
        joined_query = jnp.concatenate([query_pairs[h, p] for p in range(4)], axis=0)
        joined_grad = jnp.concatenate([grad_pairs[h, p] for p in range(4)], axis=0)
        terms = [
            gradients(
                product(key_rows, query_pairs[h, p]),
                product(value_rows, grad_pairs[h, p]),
                [penalty(listed, p, w) for w in OWN],
                finals[h, p : p + 1, :],
                finals[h, 4 + p : 5 + p, :],
            )
            for p in range(4)
        ]
        dq = [diagonal(matmul(key_turned, score_grad)) for _, score_grad in terms]
        dk = matmul(jnp.concatenate([score_grad for _, score_grad in terms], axis=1), joined_query)
        dv = matmul(jnp.concatenate([half for half, _ in terms], axis=1), joined_grad)
        for p in range(4):
            query_grad[p, :, cols(h)] = (SCALING * (dq_in[h, p] + dq[p]).T).astype(jnp.bfloat16)
        own_key[:, cols(h)] = dk
        own_value[:, cols(h)] = dv
        return carry

    lax.fori_loop(0, PAIRS, step, 0)


BF16, F32 = jnp.bfloat16, jnp.float32
TILE = (PATCH, D)
IN_VMEM = pl.BlockSpec(memory_space=pltpu.VMEM)
IN_SMEM = pl.BlockSpec(memory_space=pltpu.SMEM)


def call(kernel, outs, flops, *args):
    def space(kind):
        return IN_SMEM if kind == jnp.int32 else IN_VMEM

    return pl.pallas_call(
        kernel,
        out_shape=[jax.ShapeDtypeStruct(shape, kind) for shape, kind in outs],
        in_specs=[space(x.dtype) for x in args],
        out_specs=[space(kind) for _, kind in outs],
        compiler_params=pltpu.CompilerParams(vmem_limit_bytes=40 * 1024 * 1024),
        cost_estimate=pl.CostEstimate(flops=flops, bytes_accessed=10**6, transcendentals=0),
    )(*args)


PAIR_SHAPE = ((PAIRS, 4, 256, 128), BF16)
TURNED = ((PAIRS, 4, 128, PATCH), F32)
STATS = ((PAIRS, 8, 256), F32)
TWO = ((2, 2) + TILE, BF16)


def local(query_tiles, key_tiles, value_tiles, out_grad, mix_gain, partners, counts):
    span_total, chord_total = 2 * lax.axis_size("span"), 2 * lax.axis_size("chord")
    every = slice(None)

    def packed(tiles, *index):
        return jnp.stack([x[index] for x in tiles])

    from_up = shifted(packed((key_tiles, value_tiles), 1), 1, 0)
    from_down = shifted(packed((key_tiles, value_tiles), 0), -1, 0)
    for_left = packed((key_tiles, value_tiles, out_grad), every, 0)
    for_right = packed((key_tiles, value_tiles, out_grad), every, 1)
    from_left, from_right = shifted(for_right, 0, 1), shifted(for_left, 0, -1)

    def corners(c):
        return jnp.stack([from_up[:, c], from_down[:, c]], axis=1)

    left_corners, right_corners = corners(0), corners(1)
    corner_left = shifted(right_corners, 0, 1)
    corner_right = shifted(left_corners, 0, -1)

    key_rows, value_rows = key_tiles.reshape(4 * PATCH, D), value_tiles.reshape(4 * PATCH, D)
    listed, query_pairs, stats, attended = call(
        functools.partial(own_totals_kernel, chord_total),
        [((72,), jnp.int32), PAIR_SHAPE, STATS, TURNED], 6 * 10**9,
        partners, counts, query_tiles.reshape((4,) + TILE), key_rows, value_rows,
    )
    lower, *_ = lax.optimization_barrier((out_grad[1], for_left, for_right))
    upper, *_ = lax.optimization_barrier((out_grad[0], left_corners, right_corners))
    grad_up, grad_down = shifted(lower, 1, 0), shifted(upper, -1, 0)
    stats, attended = call(
        edge_totals_kernel, [STATS, TURNED], 6 * 10**9,
        listed, query_pairs, stats, attended, from_up, from_down, from_left, from_right,
    )
    grad_pairs, grad_turned = call(
        functools.partial(mixed_kernel, span_total, chord_total),
        [PAIR_SHAPE, ((PAIRS, 4, 128, PATCH), BF16)], 10**9,
        partners, mix_gain, out_grad, grad_up, grad_down, from_left, from_right, stats,
    )
    finals, left_back, right_back, score_grads = call(
        corner_kernel, [STATS, TWO, TWO, ((PAIRS, 4, PATCH, 256), BF16)], 2 * 10**9,
        listed, stats, attended, query_pairs, grad_pairs, grad_turned, corner_left, corner_right,
    )
    pairs = query_pairs, grad_pairs
    add_right = shifted(left_back, 0, -1)
    add_left = shifted(right_back, 0, 1)
    wide = ((2, 2) + TILE, F32)
    up_sum, down_sum, left_back, right_back, dq = call(
        edge_kernel, [wide, wide, TWO, TWO, TURNED], 8 * 10**9,
        listed, finals, *pairs, score_grads, corner_left, corner_right,
        from_up, from_down, from_left, from_right,
    )
    up_back, down_back = call(
        add_kernel, [TWO, TWO], 10**7, up_sum, down_sum, add_left, add_right
    )
    end_down = shifted(up_back, -1, 0)
    end_up = shifted(down_back, 1, 0)
    left_back, right_back, *_ = lax.optimization_barrier((left_back, right_back, up_back, down_back))
    side_right = shifted(left_back, 0, -1)
    side_left = shifted(right_back, 0, 1)
    own_key, own_value, query_grad = call(
        own_kernel, [((4 * PATCH, D), F32), ((4 * PATCH, D), F32), ((4,) + TILE, BF16)], 10**10,
        listed, finals, *pairs, key_rows, value_rows, dq,
    )

    key_grad, value_grad = call(
        last_kernel, [TWO, TWO], 10**7,
        own_key, own_value, side_left, side_right, end_up, end_down,
    )
    return (query_grad.reshape((2, 2) + TILE), key_grad, value_grad)


def solution(mesh):
    tiles = P("span", "chord", None, None)
    in_specs = (tiles, tiles, tiles, tiles, P(), P("span", "chord", None), P("span", "chord"))
    return jax.shard_map(
        local, mesh=mesh, in_specs=in_specs, out_specs=(tiles, tiles, tiles), check_vma=False
    )
```
